128 devices in a mesh: clip: 8 (over y_hi, z), seq: 16 (over x, y_lo, core).
Axes of the slice: x: 4, y: 4 (y_hi: 2, y_lo: 2; y = y_hi * 2 + y_lo), z: 4, core: 2. Of those that a mesh axis runs over, the one named last changes fastest.
Arguments:
- query_raw: bfloat16 [16384, 4096], P(('clip', 'seq')), may hold values from -400 to 400
- key_raw: bfloat16 [16384, 4096], P(('clip', 'seq')), may hold values from -400 to 400
- values: bfloat16 [16384, 4096], P(('clip', 'seq')), may hold values from -6 to 6
- query_tan: bfloat16 [16384, 4096], P(('clip', 'seq')), may hold values from -2000 to 2000
- key_tan: bfloat16 [16384, 4096], P(('clip', 'seq')), may hold values from -2000 to 2000
- values_tan: bfloat16 [16384, 4096], P(('clip', 'seq')), may hold values from -6 to 6
- query_gain: float32 [4096], P('clip'), may hold values from 0.5 to 2
- key_gain: float32 [4096], P('clip'), may hold values from 0.5 to 2
Outputs:
- attended: bfloat16 [16384, 4096], P(('clip', 'seq'))
- attended_tan: bfloat16 [16384, 4096], P(('clip', 'seq'))
The draws below stay inside these ranges and needn't reach their ends.
All inputs are finite; a program needn't handle non-finite values.
Results may differ from the reference program's by a relative error of at most 0.0163.
Values may be sent and summed in bfloat16 or wider, within the bound.
A program may use at most 64 MiB of HBM per device.

```python
import math
import jax
import jax.numpy as jnp
from jax import lax

HEADS = 32
HD = 128
WIDTH = 4096
SEQ_LEN = 2048
CLIPS = 8
TOKENS = 16384


def scale_pair(key, rows_top):
    first, second = jax.random.split(key)
    row_scale = jnp.exp(jax.random.uniform(first, (TOKENS, 1), jnp.float32) * jnp.log(rows_top))
    col_scale = jnp.exp(jax.random.uniform(second, (1, WIDTH), jnp.float32) * jnp.log(10.0))
    return (row_scale, col_scale)


def draw_query_raw(key, part):
    key = jax.random.fold_in(key, 11)
    first, second = jax.random.split(key)
    row_scale, col_scale = scale_pair(first, 10.0)
    return (jax.random.truncated_normal(second, -4.0, 4.0, (TOKENS, WIDTH), jnp.float32) * row_scale * col_scale).astype(jnp.bfloat16)


def draw_key_raw(key, part):
    key = jax.random.fold_in(key, 12)
    first, second = jax.random.split(key)
    row_scale, col_scale = scale_pair(first, 10.0)
    return (jax.random.truncated_normal(second, -4.0, 4.0, (TOKENS, WIDTH), jnp.float32) * row_scale * col_scale).astype(jnp.bfloat16)


def tangent_of(primal, key):
    first, second = jax.random.split(key)
    coef = jax.random.uniform(first, (TOKENS, 1), jnp.float32, -1.0, 1.0)
    spread = jax.random.truncated_normal(second, -4.0, 4.0, (TOKENS, WIDTH), jnp.float32)
    return coef * primal + spread * jnp.abs(primal)


def draw_query_tan(key, part):
    primal = draw_query_raw(key, part)
    key = jax.random.fold_in(key, 13)
    return tangent_of(primal, key).astype(jnp.bfloat16)


def draw_key_tan(key, part):
    primal = draw_key_raw(key, part)
    key = jax.random.fold_in(key, 14)
    return tangent_of(primal, key).astype(jnp.bfloat16)


def block_levels(stream_key, shape, cuts, smallest, largest):
    level = 1.0
    for position, parts in cuts:
        steps = jax.random.uniform(jax.random.fold_in(jax.random.fold_in(stream_key, 6), position), (parts,), jnp.float32, smallest / len(cuts), largest / len(cuts))
        level = level * jnp.repeat(jnp.exp(steps), shape[position] // parts).reshape((-1,) + (1,) * (len(shape) - 1 - position))
    return level


def normal_values(own_key, shape, scale, most, cuts=(), held_as=jnp.bfloat16):
    factor_of = block_levels(own_key, shape, cuts, -0.22, 0.18) if cuts else 1.0
    result = jax.random.normal(own_key, shape, jnp.float32) * scale * factor_of
    return jnp.minimum(jnp.maximum(result, -most), most).astype(held_as)


def setup_inputs(seed: int = 0) -> dict:
    seeds = jax.random.split(jax.random.key(seed), 9)
    query_raw = draw_query_raw(jax.random.fold_in(seeds[8], 71), 0)
    key_raw = draw_key_raw(jax.random.fold_in(seeds[8], 71), 0)
    values = normal_values(seeds[2], (TOKENS, WIDTH), 1.0, 6.0, ((0, 128),))
    query_tan = draw_query_tan(jax.random.fold_in(seeds[8], 71), 0)
    key_tan = draw_key_tan(jax.random.fold_in(seeds[8], 71), 0)
    values_tan = normal_values(seeds[5], (TOKENS, WIDTH), 1.0, 6.0, ((0, 128),))
    query_gain = jnp.clip(jnp.exp(math.log(2.0) - 1.3862944 * jax.random.uniform(seeds[6], (WIDTH,), jnp.float32) ** block_levels(seeds[6], (WIDTH,), ((0, 8),), -0.2, 0.2)), 0.5, 2.0)
    key_gain = jnp.clip(jnp.exp(math.log(2.0) - 1.3862944 * jax.random.uniform(seeds[7], (WIDTH,), jnp.float32) ** block_levels(seeds[7], (WIDTH,), ((0, 8),), -0.2, 0.2)), 0.5, 2.0)
    return {"query_raw": query_raw, "key_raw": key_raw, "values": values, "query_tan": query_tan, "key_tan": key_tan, "values_tan": values_tan, "query_gain": query_gain, "key_gain": key_gain}


epsilon = 1e-06

def normalize(raw, tangent, gain, square_sum, cross_sum, width):
    rawf = raw.astype(jnp.float32)
    tanf = tangent.astype(jnp.float32)
    root = jnp.sqrt(square_sum / width + epsilon)
    mixed = cross_sum / width
    normed = (gain * rawf / root).astype(jnp.bfloat16)
    normed_tan = (gain * (tanf / root - rawf * mixed / root ** 3)).astype(jnp.bfloat16)
    return (normed, normed_tan)

def full_norm(raw, tangent, gain):
    rawf = raw.astype(jnp.float32)
    tanf = tangent.astype(jnp.float32)
    square_sum = lax.optimization_barrier(jnp.sum(rawf * rawf, axis=-1, keepdims=True))
    cross_sum = lax.optimization_barrier(jnp.sum(rawf * tanf, axis=-1, keepdims=True))
    return normalize(raw, tangent, gain, square_sum, cross_sum, raw.shape[-1])

def product(left, right):
    return jnp.dot(left.astype(jnp.float32), right.astype(jnp.float32), precision=lax.Precision.HIGHEST)

def head_jvp(group):
    query, keys, vals, query_d, keys_d, vals_d = group
    scale = HD ** (-0.5)
    scores = product(query, keys.T) * scale
    top = lax.optimization_barrier(jnp.max(scores, axis=-1, keepdims=True))
    weights = jnp.exp(scores - top)
    weights = weights / lax.optimization_barrier(jnp.sum(weights, axis=-1, keepdims=True))
    scores_tan = (product(query_d, keys.T) + product(query, keys_d.T)) * scale
    weights_tan = weights * (scores_tan - lax.optimization_barrier(jnp.sum(weights * scores_tan, axis=-1, keepdims=True)))
    weights_low = weights.astype(jnp.bfloat16)
    weights_tan_low = weights_tan.astype(jnp.bfloat16)
    out = product(weights_low, vals).astype(jnp.bfloat16)
    out_tan = (product(weights_tan_low, vals) + product(weights_low, vals_d)).astype(jnp.bfloat16)
    return (out, out_tan)

def to_heads(array):
    return array.reshape(CLIPS, SEQ_LEN, HEADS, HD).transpose(0, 2, 1, 3).reshape(CLIPS * HEADS, SEQ_LEN, HD)

def from_heads(array):
    return array.reshape(CLIPS, HEADS, SEQ_LEN, HD).transpose(0, 2, 1, 3).reshape(TOKENS, WIDTH)

def reference(query_raw, key_raw, values, query_tan, key_tan, values_tan, query_gain, key_gain):
    query_norm, query_norm_tan = full_norm(query_raw, query_tan, query_gain)
    key_norm, key_norm_tan = full_norm(key_raw, key_tan, key_gain)
    stacked = (to_heads(query_norm), to_heads(key_norm), to_heads(values), to_heads(query_norm_tan), to_heads(key_norm_tan), to_heads(values_tan))
    outs, outs_tan = lax.map(head_jvp, stacked)
    return (from_heads(outs), from_heads(outs_tan))
```

```python
import functools

import jax
import jax.numpy as jnp
from jax import lax
from jax.experimental import pallas as pl
from jax.experimental.pallas import tpu as pltpu
from jax.sharding import PartitionSpec as P

HEADS = 32
HD = 128
EPS = 1e-06
LOG2E = 1.4426950408889634
MESH = pl.DeviceIdType.MESH
F32 = jnp.float32
BF16 = jnp.bfloat16

CHIPS = ((1, 0), (3, 0), (0, 1), (2, 0), (1, 1), (3, 1), (2, 1))
PEERS = tuple((x, y, 0) for x, y in CHIPS) + tuple((x, y, 1) for x, y in CHIPS) + ((0, 0, 1),)


def digit(table, index):
    code = sum(v * 4**i for i, v in enumerate(table))
    return (code // 4**index) % 4 if isinstance(index, int) else lax.rem(lax.shift_right_logical(jnp.int32(code), 2 * index), 4)


def kernel(clips, q_hbm, k_hbm, v_hbm, qt_hbm, kt_hbm, vt_hbm, gq_hbm, gk_hbm, o_hbm, ot_hbm,
           raw, normed, gains, vbuf, vcat, kbuf, qbuf, obuf,
           load_sem, gain_send, gain_recv, v_send, v_recv, k_send, k_recv, q_send, q_recv, o_send, o_recv):
    clip = lax.axis_index("clip")
    me = lax.axis_index("seq")
    x, y, core = me // 4, (me // 2) % 2, me % 2
    tok, width = q_hbm.shape
    groups = HEADS // 2
    length = groups * tok
    pair = 2 * HD

    def at(offset):
        return ((x + offset[0]) % 4) * 4 + ((y + offset[1]) % 2) * 2 + (core + offset[2]) % 2

    def columns(index, size):
        return pl.ds(pl.multiple_of(index * size, size), size)

    loads = [pltpu.make_async_copy(src, raw.at[i], load_sem.at[i]) for i, src in enumerate((k_hbm, kt_hbm, q_hbm, qt_hbm))]
    for copy in loads:
        copy.start()

    barrier = pltpu.get_barrier_semaphore()
    for offset in PEERS:
        pl.semaphore_signal(barrier, inc=1, device_id=(clip, at(offset)), device_id_type=MESH)
    for step in range(1, clips):
        pl.semaphore_signal(barrier, inc=1, device_id=((clip + step) % clips, me), device_id_type=MESH)
    pl.semaphore_wait(barrier, len(PEERS) + clips - 1)

    mine = columns(me, tok)
    for step in range(1, clips):
        for i, src in enumerate((gk_hbm, gq_hbm)):
            pltpu.make_async_remote_copy(
                src_ref=src, dst_ref=gains.at[i, clip], send_sem=gain_send.at[i], recv_sem=gain_recv,
                device_id=((clip + step) % clips, me), device_id_type=MESH).start()
    for offset in PEERS:
        to = at(offset)
        for i, src in enumerate((v_hbm, vt_hbm)):
            pltpu.make_async_remote_copy(
                src_ref=src.at[:, columns(to, pair)], dst_ref=vbuf.at[i, mine, :], send_sem=v_send.at[i], recv_sem=v_recv,
                device_id=(clip, to), device_id_type=MESH).start()
    for i, src in enumerate((gk_hbm, gq_hbm)):
        pltpu.make_async_copy(src, gains.at[i, clip], gain_recv).start()
    for i, src in enumerate((v_hbm, vt_hbm)):
        pltpu.make_async_copy(src.at[:, columns(me, pair)], vbuf.at[i, mine, :], v_recv).start()
    pltpu.make_async_copy(gains, gains, gain_recv).wait()

    def norm(i, tangent_first):
        first, second = (1, 0) if tangent_first else (0, 1)

        def rows(n, _):
            r = pl.ds(pl.multiple_of(n * 16, 16), 16)
            square, cross = jnp.zeros((16, HD), F32), jnp.zeros((16, HD), F32)
            for h in range(HEADS):
                a = raw[2 * i, r, h * HD:(h + 1) * HD].astype(F32)
                b = raw[2 * i + 1, r, h * HD:(h + 1) * HD].astype(F32)
                square += a * a
                cross += a * b
            inverse = 1.0 / jnp.sqrt(jnp.sum(square, axis=1, keepdims=True) / width + EPS)
            mixed = jnp.sum(cross, axis=1, keepdims=True) / width * (inverse * inverse * inverse)
            per = gains.shape[-1] // HD
            for h in range(HEADS):
                a = raw[2 * i, r, h * HD:(h + 1) * HD].astype(F32)
                b = raw[2 * i + 1, r, h * HD:(h + 1) * HD].astype(F32)
                g = gains[i, h // per, :, (h % per) * HD:(h % per + 1) * HD]
                normed[i, r, (2 * h + first) * HD:(2 * h + first + 1) * HD] = (g * a * inverse).astype(BF16)
                normed[i, r, (2 * h + second) * HD:(2 * h + second + 1) * HD] = (g * (b * inverse - a * mixed)).astype(BF16)
            return 0

        lax.fori_loop(0, tok // 16, rows, 0)

    loads[0].wait()
    loads[1].wait()
    norm(0, False)
    for offset in PEERS:
        to = at(offset)
        pltpu.make_async_remote_copy(
            src_ref=normed.at[0, :, columns(to, 2 * pair)], dst_ref=kbuf.at[mine, :], send_sem=k_send, recv_sem=k_recv,
            device_id=(clip, to), device_id_type=MESH).start()
    pltpu.make_async_copy(normed.at[0, :, columns(me, 2 * pair)], kbuf.at[mine, :], k_recv).start()
    loads[2].wait()
    loads[3].wait()
    norm(1, True)
    for offset in PEERS:
        to = at(offset)
        pltpu.make_async_remote_copy(
            src_ref=normed.at[1, :, columns(to, 2 * pair)], dst_ref=qbuf.at[mine, :], send_sem=q_send, recv_sem=q_recv.at[me],
            device_id=(clip, to), device_id_type=MESH).start()
    pltpu.make_async_copy(normed.at[1, :, columns(me, 2 * pair)], qbuf.at[mine, :], q_recv.at[me]).start()

    pltpu.make_async_copy(vbuf, vbuf, v_recv).wait()

    def interleave(n, _):
        r = pl.ds(pl.multiple_of(n * 128, 128), 128)
        for h in range(2):
            for i in range(2):
                vcat[r, (2 * h + i) * HD:(2 * h + i + 1) * HD] = vbuf[i, r, h * HD:(h + 1) * HD]
        return 0

    lax.fori_loop(0, length // 128, interleave, 0)
    pltpu.make_async_copy(kbuf, kbuf, k_recv).wait()

    scale = HD ** (-0.5)
    order = tuple(((4 - dx) % 4, dy) for dx, dy in CHIPS) + ((0, 0),)

    def attend(t, _):
        chip = ((x + digit([o[0] for o in order], t)) % 4) * 2 + (y + digit([o[1] for o in order], t)) % 2
        r = pl.ds(pl.multiple_of(chip * 2 * tok, 2 * tok), 2 * tok)
        for c in range(2):
            owner = chip * 2 + c
            block = qbuf.at[columns(owner, tok), :]
            pltpu.make_async_copy(block, block, q_recv.at[owner]).wait()
        for h in range(2):
            cols = slice(h * pair, (h + 1) * pair)
            queries = qbuf[r, cols]
            keys = kbuf[:, cols]
            dims = (((1,), (1,)), ((), ()))
            scores = lax.dot_general(queries[:, HD:], keys[:, :HD], dims, preferred_element_type=F32)
            scores_tan = lax.dot_general(queries, keys, dims, preferred_element_type=F32)
            top = jnp.max(scores, axis=1, keepdims=True)
            weights = jnp.exp2((scores - top) * (scale * LOG2E))
            inverse = 1.0 / jnp.sum(weights, axis=1, keepdims=True)
            mean = jnp.sum(weights * scores_tan, axis=1, keepdims=True) * inverse
            low = (weights * inverse).astype(BF16)
            low_tan = (weights * (scores_tan - mean) * (inverse * scale)).astype(BF16)
            both = jnp.dot(low, vcat[:, cols], preferred_element_type=F32)
            rest = jnp.dot(low_tan, vcat[:, h * pair:h * pair + HD], preferred_element_type=F32)
            obuf[0, r, h * HD:(h + 1) * HD] = both[:, :HD].astype(BF16)
            obuf[1, r, h * HD:(h + 1) * HD] = (both[:, HD:] + rest).astype(BF16)
        for c in range(2):
            owner = chip * 2 + c
            for i, out in enumerate((o_hbm, ot_hbm)):
                block = obuf.at[i, columns(owner, tok), :]
                place = out.at[:, columns(me, pair)]

                @pl.when(owner != me)
                def _():
                    pltpu.make_async_remote_copy(
                        src_ref=block, dst_ref=place, send_sem=o_send.at[i], recv_sem=o_recv.at[i],
                        device_id=(clip, owner), device_id_type=MESH).start()

                @pl.when(owner == me)
                def _():
                    pltpu.make_async_copy(block, place, o_recv.at[i]).start()
        return 0

    lax.fori_loop(0, groups // 2, attend, 0)

    for i, out in enumerate((o_hbm, ot_hbm)):
        pltpu.make_async_copy(out, out, o_recv.at[i]).wait()
    others = pl.ds(0, length - tok)
    for i in range(2):
        pltpu.make_async_copy(vbuf.at[i, others, :], vbuf.at[i, others, :], v_send.at[i]).wait()
        pltpu.make_async_copy(obuf.at[i, others, :], obuf.at[i, others, :], o_send.at[i]).wait()
        pltpu.make_async_copy(gains.at[i, pl.ds(0, clips - 1)], gains.at[i, pl.ds(0, clips - 1)], gain_send.at[i]).wait()
    pltpu.make_async_copy(kbuf.at[others, :], kbuf.at[others, :], k_send).wait()
    pltpu.make_async_copy(qbuf.at[others, :], qbuf.at[others, :], q_send).wait()


def on_device(query_raw, key_raw, values, query_tan, key_tan, values_tan, query_gain, key_gain):
    tok, width = query_raw.shape
    groups = lax.axis_size("seq")
    clips = lax.axis_size("clip")
    length = tok * groups
    share = query_gain.shape[0]
    dma = pltpu.SemaphoreType.DMA
    anywhere = pl.BlockSpec(memory_space=pl.ANY)
    return pl.pallas_call(
        functools.partial(kernel, clips),
        out_shape=(jax.ShapeDtypeStruct((tok, width), BF16),) * 2,
        in_specs=[anywhere] * 8,
        out_specs=(anywhere,) * 2,
        scratch_shapes=[
            pltpu.VMEM((4, tok, width), BF16),
            pltpu.VMEM((2, tok, 2 * width), BF16),
            pltpu.VMEM((2, clips, 1, share), F32),
            pltpu.VMEM((2, length, 2 * HD), BF16),
            pltpu.VMEM((length, 4 * HD), BF16),
            pltpu.VMEM((length, 4 * HD), BF16),
            pltpu.VMEM((length, 4 * HD), BF16),
            pltpu.VMEM((2, length, 2 * HD), BF16),
            dma((4,)), dma((2,)), dma, dma((2,)), dma, dma, dma, dma, dma((groups,)), dma((2,)), dma((2,)),
        ],
        compiler_params=pltpu.CompilerParams(
            collective_id=0, has_side_effects=True, vmem_limit_bytes=56 * 2**20
        ),
        cost_estimate=pl.CostEstimate(flops=13_000_000_000, bytes_accessed=8 * 2**20, transcendentals=8_400_000),
    )(query_raw, key_raw, values, query_tan, key_tan, values_tan,
      query_gain.reshape(1, share), key_gain.reshape(1, share))


def solution(mesh):
    tokens = P(("clip", "seq"), None)
    return jax.shard_map(
        on_device, mesh=mesh, in_specs=(tokens,) * 6 + (P("clip"),) * 2, out_specs=(tokens,) * 2, check_vma=False
    )
```

```python
import functools

import jax
import jax.numpy as jnp
from jax import lax
from jax.experimental import pallas as pl
from jax.experimental.pallas import tpu as pltpu
from jax.sharding import PartitionSpec as P

HEADS = 32
HD = 128
EPS = 1e-06
LOG2E = 1.4426950408889634
MESH = pl.DeviceIdType.MESH
F32 = jnp.float32
BF16 = jnp.bfloat16

NEAR = ((1, 0), (3, 0), (0, 1), (2, 0))
FAR = ((1, 1), (3, 1), (2, 1), (0, 0))
PLACES = tuple((dx, dy, core) for chips in (NEAR, FAR) for core in range(2) for dx, dy in chips)
OWN = PLACES.index((0, 0, 0))
OTHERS = tuple(p for p in range(16) if p != OWN)
PARTS = 2
CHUNKS = 4


def kernel(clips, q_hbm, k_hbm, v_hbm, qt_hbm, kt_hbm, vt_hbm, gq_hbm, gk_hbm, out_hbm,
           raw, normed, gains, vbuf, vcat, kbuf, qbuf, obuf,
           load_sem, gain_send, gain_recv, v_send, v_recv, k_send, k_recv, q_send, q_recv, o_send, o_recv):
    clip = lax.axis_index("clip")
    me = lax.axis_index("seq")
    x, y, core = me // 4, (me // 2) % 2, me % 2
    way = 1 - 2 * (x % 2)
    tok, width = q_hbm.shape
    groups = HEADS // 2
    length = groups * tok
    pair = 2 * HD
    piece = tok // PARTS

    def at(place):
        dx, dy, other = PLACES[place]
        return ((x + way * dx + 4) % 4) * 4 + ((y + dy) % 2) * 2 + (core + other) % 2

    def columns(index, size):
        return pl.ds(pl.multiple_of(index * size, size), size)

    loads = [pltpu.make_async_copy(src, raw.at[i], load_sem.at[i]) for i, src in enumerate((k_hbm, kt_hbm, q_hbm, qt_hbm))]
    for copy in loads:
        copy.start()

    barrier = pltpu.get_barrier_semaphore()
    for place in OTHERS:
        pl.semaphore_signal(barrier, inc=1, device_id=(clip, at(place)), device_id_type=MESH)
    for step in range(1, clips):
        pl.semaphore_signal(barrier, inc=1, device_id=((clip + step) % clips, me), device_id_type=MESH)
    pl.semaphore_wait(barrier, len(OTHERS) + clips - 1)

    for step in range(1, clips):
        for i, src in enumerate((gk_hbm, gq_hbm)):
            pltpu.make_async_remote_copy(
                src_ref=src, dst_ref=gains.at[i, clip], send_sem=gain_send.at[i], recv_sem=gain_recv,
                device_id=((clip + step) % clips, me), device_id_type=MESH).start()
    for i, src in enumerate((v_hbm, vt_hbm)):
        for place in OTHERS:
            to = at(place)
            pltpu.make_async_remote_copy(
                src_ref=src.at[:, columns(to, pair)], dst_ref=vbuf.at[i, pl.ds(place * tok, tok), :], send_sem=v_send.at[i], recv_sem=v_recv,
                device_id=(clip, to), device_id_type=MESH).start()
    for i, src in enumerate((gk_hbm, gq_hbm)):
        pltpu.make_async_copy(src, gains.at[i, clip], gain_recv).start()
    for i, src in enumerate((v_hbm, vt_hbm)):
        pltpu.make_async_copy(src.at[:, columns(me, pair)], vbuf.at[i, pl.ds(OWN * tok, tok), :], v_recv).start()
    pltpu.make_async_copy(gains, gains, gain_recv).wait()

    def norm(i, tangent_first):
        first, second = (1, 0) if tangent_first else (0, 1)

        def rows(n, _):
            r = pl.ds(pl.multiple_of(n * 16, 16), 16)
            square, cross = jnp.zeros((16, HD), F32), jnp.zeros((16, HD), F32)
            for h in range(HEADS):
                a = raw[2 * i, r, h * HD:(h + 1) * HD].astype(F32)
                b = raw[2 * i + 1, r, h * HD:(h + 1) * HD].astype(F32)
                square += a * a
                cross += a * b
            inverse = 1.0 / jnp.sqrt(jnp.sum(square, axis=1, keepdims=True) / width + EPS)
            mixed = jnp.sum(cross, axis=1, keepdims=True) / width * (inverse * inverse * inverse)
            per = gains.shape[-1] // HD
            for h in range(HEADS):
                a = raw[2 * i, r, h * HD:(h + 1) * HD].astype(F32)
                b = raw[2 * i + 1, r, h * HD:(h + 1) * HD].astype(F32)
                g = gains[i, h // per, :, (h % per) * HD:(h % per + 1) * HD]
                normed[i, r, (2 * h + first) * HD:(2 * h + first + 1) * HD] = (g * a * inverse).astype(BF16)
                normed[i, r, (2 * h + second) * HD:(2 * h + second + 1) * HD] = (g * (b * inverse - a * mixed)).astype(BF16)
            return 0

        lax.fori_loop(0, tok // 16, rows, 0)

    loads[0].wait()
    loads[1].wait()
    norm(0, False)
    for head in range(2):
        for place in OTHERS:
            to = at(place)
            pltpu.make_async_remote_copy(
                src_ref=normed.at[0, :, columns(2 * to + head, pair)], dst_ref=kbuf.at[head, pl.ds(place * tok, tok), :],
                send_sem=k_send, recv_sem=k_recv, device_id=(clip, to), device_id_type=MESH).start()
    for head in range(2):
        pltpu.make_async_copy(
            normed.at[0, :, columns(2 * me + head, pair)], kbuf.at[head, pl.ds(OWN * tok, tok), :], k_recv).start()
    loads[2].wait()
    loads[3].wait()
    norm(1, True)
    for part in range(PARTS):
        rows = pl.ds(part * piece, piece)
        for place in range(16):
            to = at(place)
            block = normed.at[1, rows, columns(to, 2 * pair)]
            there = qbuf.at[part, place // 4, pl.ds(place % 4 * piece, piece), :]
            if place == OWN:
                pltpu.make_async_copy(block, there, q_recv.at[part, place]).start()
            else:
                pltpu.make_async_remote_copy(
                    src_ref=block, dst_ref=there, send_sem=q_send, recv_sem=q_recv.at[part, place],
                    device_id=(clip, to), device_id_type=MESH).start()

    pltpu.make_async_copy(vbuf, vbuf, v_recv).wait()

    def interleave(n, _):
        r = pl.ds(pl.multiple_of(n * 128, 128), 128)
        for h in range(2):
            for i in range(2):
                vcat[r, (2 * h + i) * HD:(2 * h + i + 1) * HD] = vbuf[i, r, h * HD:(h + 1) * HD]
        return 0

    lax.fori_loop(0, length // 128, interleave, 0)
    pltpu.make_async_copy(kbuf, kbuf, k_recv).wait()

    scale = HD ** (-0.5)
    def attend(step, _):
        part, group = step // 4, step % 4
        for n in range(4):
            block = qbuf.at[part, group, pl.ds(n * piece, piece), :]
            pltpu.make_async_copy(block, block, q_recv.at[part, group * 4 + n]).wait()
        for h in range(2):
            queries = qbuf[part, group, :, h * pair:(h + 1) * pair]
            keys = kbuf[h]
            dims = (((1,), (1,)), ((), ()))
            scores = lax.dot_general(queries[:, HD:], keys[:, :HD], dims, preferred_element_type=F32)
            scores_tan = lax.dot_general(queries, keys, dims, preferred_element_type=F32)
            top = jnp.max(scores, axis=1, keepdims=True)
            weights = jnp.exp2((scores - top) * (scale * LOG2E))
            inverse = 1.0 / jnp.sum(weights, axis=1, keepdims=True)
            mean = jnp.sum(weights * scores_tan, axis=1, keepdims=True) * inverse
            low = (weights * inverse).astype(BF16)
            low_tan = (weights * (scores_tan - mean) * (inverse * scale)).astype(BF16)
            both = jnp.dot(low, vcat[:, h * pair:(h + 1) * pair], preferred_element_type=F32)
            rest = jnp.dot(low_tan, vcat[:, h * pair:h * pair + HD], preferred_element_type=F32)
            obuf[step, 0, :, h * HD:(h + 1) * HD] = both[:, :HD].astype(BF16)
            obuf[step, 1, :, h * HD:(h + 1) * HD] = (both[:, HD:] + rest).astype(BF16)
        far, other = group // 2, group % 2
        rows = pl.ds(pl.multiple_of(part * piece, piece), piece)
        for n in range(4):
            dx = NEAR[n][0] + far * (FAR[n][0] - NEAR[n][0])
            dy = NEAR[n][1] + far * (FAR[n][1] - NEAR[n][1])
            owner = ((x + way * dx + 4) % 4) * 4 + ((y + dy) % 2) * 2 + (core + other) % 2
            block = obuf.at[step, :, pl.ds(n * piece, piece), :]
            there = out_hbm.at[:, rows, columns(me, pair)]

            def send(block=block, there=there, owner=owner):
                pltpu.make_async_remote_copy(
                    src_ref=block, dst_ref=there, send_sem=o_send, recv_sem=o_recv,
                    device_id=(clip, owner), device_id_type=MESH).start()

            if n == OWN % 4:
                pl.when(group != OWN // 4)(send)

                @pl.when(group == OWN // 4)
                def _():
                    pltpu.make_async_copy(block, there, o_recv).start()
            else:
                send()
        return 0

    lax.fori_loop(0, PARTS * 4, attend, 0)

    pltpu.make_async_copy(out_hbm, out_hbm, o_recv).wait()
    others = pl.ds(0, length - tok)
    for i in range(2):
        pltpu.make_async_copy(vbuf.at[i, others, :], vbuf.at[i, others, :], v_send.at[i]).wait()
        pltpu.make_async_copy(gains.at[i, pl.ds(0, clips - 1)], gains.at[i, pl.ds(0, clips - 1)], gain_send.at[i]).wait()
    pltpu.make_async_copy(kbuf.at[:, others, :], kbuf.at[:, others, :], k_send).wait()
    most = pl.ds(0, 4 * piece - piece // 4)
    pltpu.make_async_copy(qbuf.at[:, :, most, :], qbuf.at[:, :, most, :], q_send).wait()
    pltpu.make_async_copy(obuf.at[:, :, most, :], obuf.at[:, :, most, :], o_send).wait()


def hand_out(both, first, second, buf, in_sems, out_sems):
    pieces, rows = buf.shape[0] // 2, buf.shape[1]
    copies = []
    for n in range(pieces):
        for i, out in enumerate((first, second)):
            k, r = 2 * n + i, pl.ds(n * rows, rows)
            copies.append((pltpu.make_async_copy(both.at[i, r, :], buf.at[k], in_sems.at[k]),
                           pltpu.make_async_copy(buf.at[k], out.at[r, :], out_sems.at[k])))
    for fetch, _ in copies:
        fetch.start()
    for fetch, store in copies:
        fetch.wait()
        store.start()
    for _, store in copies:
        store.wait()


def on_device(query_raw, key_raw, values, query_tan, key_tan, values_tan, query_gain, key_gain):
    tok, width = query_raw.shape
    groups = lax.axis_size("seq")
    clips = lax.axis_size("clip")
    length = tok * groups
    share = query_gain.shape[0]
    dma = pltpu.SemaphoreType.DMA
    anywhere = pl.BlockSpec(memory_space=pl.ANY)
    both = pl.pallas_call(
        functools.partial(kernel, clips),
        out_shape=jax.ShapeDtypeStruct((2, tok, width), BF16),
        in_specs=[anywhere] * 8,
        out_specs=anywhere,
        scratch_shapes=[
            pltpu.VMEM((4, tok, width), BF16),
            pltpu.VMEM((2, tok, 2 * width), BF16),
            pltpu.VMEM((2, clips, 1, share), F32),
            pltpu.VMEM((2, length, 2 * HD), BF16),
            pltpu.VMEM((length, 4 * HD), BF16),
            pltpu.VMEM((2, length, 2 * HD), BF16),
            pltpu.VMEM((PARTS, 4, length // PARTS // 4, 4 * HD), BF16),
            pltpu.VMEM((PARTS * 4, 2, length // PARTS // 4, 2 * HD), BF16),
            dma((4,)), dma((2,)), dma, dma((2,)), dma, dma, dma, dma, dma((PARTS, groups)), dma, dma,
        ],
        compiler_params=pltpu.CompilerParams(
            collective_id=0, has_side_effects=True, vmem_limit_bytes=56 * 2**20
        ),
        cost_estimate=pl.CostEstimate(flops=13_000_000_000, bytes_accessed=8 * 2**20, transcendentals=8_400_000),
    )(query_raw, key_raw, values, query_tan, key_tan, values_tan,
      query_gain.reshape(1, share), key_gain.reshape(1, share))
    return pl.pallas_call(
        hand_out,
        out_shape=(jax.ShapeDtypeStruct((tok, width), BF16),) * 2,
        in_specs=[anywhere],
        out_specs=(anywhere,) * 2,
        scratch_shapes=[pltpu.VMEM((2 * CHUNKS, tok // CHUNKS, width), BF16), dma((2 * CHUNKS,)), dma((2 * CHUNKS,))],
    )(both)


def solution(mesh):
    tokens = P(("clip", "seq"), None)
    return jax.shard_map(
        on_device, mesh=mesh, in_specs=(tokens,) * 6 + (P("clip"),) * 2, out_specs=(tokens,) * 2, check_vma=False
    )
```

```python
import functools

import jax
import jax.numpy as jnp
from jax import lax
from jax.experimental import pallas as pl
from jax.experimental.pallas import tpu as pltpu
from jax.sharding import PartitionSpec as P

HEADS = 32
HD = 128
EPS = 1e-06
LOG2E = 1.4426950408889634
MESH = pl.DeviceIdType.MESH
F32 = jnp.float32
BF16 = jnp.bfloat16

FAR = ((2, 1), (3, 1), (1, 1), (0, 0))
NEAR = ((0, 1), (2, 0), (3, 0), (1, 0))
PLACES = tuple((dx, dy, core) for core in range(2) for chips in (FAR, NEAR) for dx, dy in chips)
OWN = PLACES.index((0, 0, 0))
OTHERS = tuple(p for p in range(16) if p != OWN)
PARTS = 2
RELAY = 0


def kernel(clips, q_hbm, k_hbm, v_hbm, qt_hbm, kt_hbm, vt_hbm, gq_hbm, gk_hbm, out_hbm,
           queries, keys, figures, figure_mine, figure_all, figure_of, gains, gain,
           vbuf, vcat, kraw, kbuf, qbuf, obuf,
           load_k, load_q, gain_send, gain_recv, hand_send, hand_recv, figure_send, figure_recv,
           v_send, v_recv, k_send, k_recv, q_send, q_recv, o_send, o_recv):
    clip = lax.axis_index("clip")
    me = lax.axis_index("seq")
    x, y, core = me // 4, (me // 2) % 2, me % 2
    way = 1 - 2 * (x % 2)
    tok, width = q_hbm.shape
    groups = HEADS // 2
    length = groups * tok
    pair = 2 * HD
    piece = tok // PARTS
    share = gains.shape[-1]

    def at(place):
        dx, dy, other = PLACES[place]
        return ((x + way * dx + 4) % 4) * 4 + ((y + dy) % 2) * 2 + (core + other) % 2

    def columns(index, size):
        return pl.ds(pl.multiple_of(index * size, size), size)

    def send(src, dst, send_sem, recv_sem, to):
        pltpu.make_async_remote_copy(
            src_ref=src, dst_ref=dst, send_sem=send_sem, recv_sem=recv_sem, device_id=(clip, to), device_id_type=MESH).start()

    for i, src in enumerate((k_hbm, kt_hbm)):
        pltpu.make_async_copy(src, keys.at[i], load_k).start()
    for n in range(groups):
        for i, src in enumerate((qt_hbm, q_hbm)):
            pltpu.make_async_copy(
                src.at[:, n * pair:(n + 1) * pair], queries.at[:, (2 * n + i) * pair:(2 * n + i + 1) * pair], load_q).start()

    barrier = pltpu.get_barrier_semaphore()
    for place in OTHERS:
        pl.semaphore_signal(barrier, inc=1, device_id=(clip, at(place)), device_id_type=MESH)

    @pl.when(me == RELAY)
    def _():
        for step in range(1, clips):
            pl.semaphore_signal(barrier, inc=1, device_id=((clip + step) % clips, me), device_id_type=MESH)

    @pl.when(me != RELAY)
    def _():
        pl.semaphore_wait(barrier, len(OTHERS))

    @pl.when(me == RELAY)
    def _():
        pl.semaphore_wait(barrier, len(OTHERS) + clips - 1)
        for i, src in enumerate((gk_hbm, gq_hbm)):
            for step in range(1, clips):
                pltpu.make_async_remote_copy(
                    src_ref=src, dst_ref=gains.at[i, clip], send_sem=gain_send.at[i], recv_sem=gain_recv,
                    device_id=((clip + step) % clips, me), device_id_type=MESH).start()
            pltpu.make_async_copy(src, gains.at[i, clip], gain_recv).start()

    for i, src in enumerate((v_hbm, vt_hbm)):
        for place in OTHERS:
            to = at(place)
            send(src.at[:, columns(to, pair)], vbuf.at[i, pl.ds(place * tok, tok), :], v_send.at[i], v_recv, to)
        pltpu.make_async_copy(src.at[:, columns(me, pair)], vbuf.at[i, pl.ds(OWN * tok, tok), :], v_recv).start()

    pltpu.make_async_copy(keys, keys, load_k).wait()
    pltpu.make_async_copy(queries, queries, load_q).wait()

    def token_figures(n, _):
        r = pl.ds(pl.multiple_of(n * 16, 16), 16)

        def pair_of(primal, tangent):
            square, cross = jnp.zeros((16, HD), F32), jnp.zeros((16, HD), F32)
            for h in range(HEADS):
                a, b = primal(h).astype(F32), tangent(h).astype(F32)
                square += a * a
                cross += a * b
            inverse = 1.0 / jnp.sqrt(jnp.sum(square, axis=1, keepdims=True) / width + EPS)
            return inverse, jnp.sum(cross, axis=1, keepdims=True) / width * (inverse * inverse * inverse)

        def query_part(i):
            def part(h):
                start = (2 * (h // 2) + i) * pair + h % 2 * HD
                return queries[r, start:start + HD]
            return part

        found = pair_of(query_part(1), query_part(0)) + pair_of(
            lambda h: keys[0, r, h * HD:(h + 1) * HD], lambda h: keys[1, r, h * HD:(h + 1) * HD])
        lane = lax.broadcasted_iota(jnp.int32, (16, HD), 1)
        row = jnp.zeros((16, HD), F32)
        for i, value in enumerate(found):
            row = jnp.where(lane == i, value, row)
        figures[r, :] = row
        return 0

    lax.fori_loop(0, tok // 16, token_figures, 0)
    figure_mine[...] = figures[...].T[:8, :]
    for place in OTHERS:
        send(figure_mine, figure_all.at[place], figure_send, figure_recv, at(place))
    pltpu.make_async_copy(figure_mine, figure_all.at[OWN], figure_recv).start()

    def gain_part(to):
        return gains.at[:, to // (share // pair), :, pl.ds(pl.multiple_of(to % (share // pair) * pair, pair), pair)]

    @pl.when(me == RELAY)
    def _():
        pltpu.make_async_copy(gains, gains, gain_recv).wait()
        for place in OTHERS:
            to = at(place)
            send(gain_part(to), gain, hand_send.at[place], hand_recv, to)
        pltpu.make_async_copy(gain_part(me), gain, hand_recv).start()

    for i in range(2):
        for place in OTHERS:
            to = at(place)
            send(keys.at[i, :, columns(to, pair)], kraw.at[i, pl.ds(place * tok, tok), :], k_send.at[i], k_recv, to)
        pltpu.make_async_copy(keys.at[i, :, columns(me, pair)], kraw.at[i, pl.ds(OWN * tok, tok), :], k_recv).start()
    for part in range(PARTS):
        rows = pl.ds(part * piece, piece)
        for place in range(16):
            to = at(place)
            block = queries.at[rows, columns(to, 2 * pair)]
            there = qbuf.at[part, place // 4, pl.ds(place % 4 * piece, piece), :]
            if place == OWN:
                pltpu.make_async_copy(block, there, q_recv.at[part, place]).start()
            else:
                send(block, there, q_send, q_recv.at[part, place], to)

    pltpu.make_async_copy(vbuf, vbuf, v_recv).wait()

    def interleave(n, _):
        r = pl.ds(pl.multiple_of(n * 128, 128), 128)
        for h in range(2):
            for i in range(2):
                vcat[r, (2 * h + i) * HD:(2 * h + i + 1) * HD] = vbuf[i, r, h * HD:(h + 1) * HD]
        return 0

    lax.fori_loop(0, length // 128, interleave, 0)
    pltpu.make_async_copy(figure_all, figure_all, figure_recv).wait()

    def upright(place, _):
        figure_of[place] = figure_all[place].T
        return 0

    lax.fori_loop(0, groups, upright, 0)
    pltpu.make_async_copy(gain, gain, hand_recv).wait()
    pltpu.make_async_copy(kraw, kraw, k_recv).wait()

    def norm(a, b, g, inverse, mixed):
        a, b = a.astype(F32), b.astype(F32)
        return (g * a * inverse).astype(BF16), (g * (b * inverse - a * mixed)).astype(BF16)

    def norm_keys(place, _):
        r = pl.ds(pl.multiple_of(place * tok, tok), tok)
        inverse, mixed = figure_of[place, :, 2:3], figure_of[place, :, 3:4]
        for h in range(2):
            cols = slice(h * HD, (h + 1) * HD)
            primal, tangent = norm(kraw[0, r, cols], kraw[1, r, cols], gain[0, :, cols], inverse, mixed)
            kbuf[h, r, :HD] = primal
            kbuf[h, r, HD:] = tangent
        return 0

    lax.fori_loop(0, groups, norm_keys, 0)

    scale = HD ** (-0.5)

    def attend(step, _):
        part, group = step // 4, step % 4
        rows = pl.ds(pl.multiple_of(part * piece, piece), piece)
        for n in range(4):
            block = qbuf.at[part, group, pl.ds(n * piece, piece), :]
            pltpu.make_async_copy(block, block, q_recv.at[part, group * 4 + n]).wait()
        for h in range(2):
            primal, tangent = [], []
            for n in range(4):
                own = figure_of.at[group * 4 + n]
                p, t = norm(
                    qbuf[part, group, n * piece:(n + 1) * piece, pair + h * HD:pair + (h + 1) * HD],
                    qbuf[part, group, n * piece:(n + 1) * piece, h * HD:(h + 1) * HD],
                    gain[1, :, h * HD:(h + 1) * HD], own[rows, 0:1], own[rows, 1:2])
                primal.append(p)
                tangent.append(t)
            primal, tangent = jnp.concatenate(primal, axis=0), jnp.concatenate(tangent, axis=0)
            both_keys = kbuf[h]
            dims = (((1,), (1,)), ((), ()))
            scores = lax.dot_general(primal, both_keys[:, :HD], dims, preferred_element_type=F32)
            scores_tan = lax.dot_general(
                jnp.concatenate([tangent, primal], axis=1), both_keys, dims, preferred_element_type=F32)
            top = jnp.max(scores, axis=1, keepdims=True)
            weights = jnp.exp2((scores - top) * (scale * LOG2E))
            inverse = 1.0 / jnp.sum(weights, axis=1, keepdims=True)
            mean = jnp.sum(weights * scores_tan, axis=1, keepdims=True) * inverse
            low = (weights * inverse).astype(BF16)
            low_tan = (weights * (scores_tan - mean) * (inverse * scale)).astype(BF16)
            both = jnp.dot(low, vcat[:, h * pair:(h + 1) * pair], preferred_element_type=F32)
            rest = jnp.dot(low_tan, vcat[:, h * pair:h * pair + HD], preferred_element_type=F32)
            obuf[step, 0, :, h * HD:(h + 1) * HD] = both[:, :HD].astype(BF16)
            obuf[step, 1, :, h * HD:(h + 1) * HD] = (both[:, HD:] + rest).astype(BF16)
        other, near = group // 2, group % 2
        for n in range(4):
            dx = FAR[n][0] + near * (NEAR[n][0] - FAR[n][0])
            dy = FAR[n][1] + near * (NEAR[n][1] - FAR[n][1])
            owner = ((x + way * dx + 4) % 4) * 4 + ((y + dy) % 2) * 2 + (core + other) % 2
            block = obuf.at[step, :, pl.ds(n * piece, piece), :]
            there = out_hbm.at[:, rows, columns(me, pair)]
            give = functools.partial(send, block, there, o_send, o_recv, owner)
            if n == OWN % 4:
                pl.when(group != OWN // 4)(give)

                @pl.when(group == OWN // 4)
                def _():
                    pltpu.make_async_copy(block, there, o_recv).start()
            else:
                give()
        return 0

    lax.fori_loop(0, PARTS * 4, attend, 0)

    pltpu.make_async_copy(out_hbm, out_hbm, o_recv).wait()
    others = pl.ds(0, length - tok)
    for i in range(2):
        pltpu.make_async_copy(vbuf.at[i, others, :], vbuf.at[i, others, :], v_send.at[i]).wait()
        pltpu.make_async_copy(kraw.at[i, others, :], kraw.at[i, others, :], k_send.at[i]).wait()
    pltpu.make_async_copy(figure_all.at[pl.ds(0, groups - 1)], figure_all.at[pl.ds(0, groups - 1)], figure_send).wait()
    most = pl.ds(0, 4 * piece - piece // 4)
    pltpu.make_async_copy(qbuf.at[:, :, most, :], qbuf.at[:, :, most, :], q_send).wait()
    pltpu.make_async_copy(obuf.at[:, :, most, :], obuf.at[:, :, most, :], o_send).wait()

    @pl.when(me == RELAY)
    def _():
        for i in range(2):
            pltpu.make_async_copy(gains.at[i, pl.ds(0, clips - 1)], gains.at[i, pl.ds(0, clips - 1)], gain_send.at[i]).wait()
        for place in OTHERS:
            pltpu.make_async_copy(gain, gain, hand_send.at[place]).wait()


def hand_out(both, first, second, sems):
    copies = [pltpu.make_async_copy(both.at[i], out, sems.at[i]) for i, out in enumerate((first, second))]
    for copy in copies:
        copy.start()
    for copy in copies:
        copy.wait()


def on_device(query_raw, key_raw, values, query_tan, key_tan, values_tan, query_gain, key_gain):
    tok, width = query_raw.shape
    groups = lax.axis_size("seq")
    clips = lax.axis_size("clip")
    length = tok * groups
    share = query_gain.shape[0]
    pair = 2 * HD
    dma = pltpu.SemaphoreType.DMA
    anywhere = pl.BlockSpec(memory_space=pl.ANY)
    both = pl.pallas_call(
        functools.partial(kernel, clips),
        out_shape=pltpu.VMEM((2, tok, width), BF16),
        in_specs=[anywhere] * 8,
        out_specs=pl.BlockSpec(memory_space=pltpu.VMEM),
        scratch_shapes=[
            pltpu.VMEM((tok, 2 * width), BF16),
            pltpu.VMEM((2, tok, width), BF16),
            pltpu.VMEM((tok, HD), F32),
            pltpu.VMEM((8, tok), F32),
            pltpu.VMEM((groups, 8, tok), F32),
            pltpu.VMEM((groups, tok, 8), F32),
            pltpu.VMEM((2, clips, 1, share), F32),
            pltpu.VMEM((2, 1, pair), F32),
            pltpu.VMEM((2, length, pair), BF16),
            pltpu.VMEM((length, 2 * pair), BF16),
            pltpu.VMEM((2, length, pair), BF16),
            pltpu.VMEM((2, length, pair), BF16),
            pltpu.VMEM((PARTS, 4, length // PARTS // 4, 2 * pair), BF16),
            pltpu.VMEM((PARTS * 4, 2, length // PARTS // 4, pair), BF16),
            dma, dma, dma((2,)), dma, dma((groups,)), dma, dma, dma,
            dma((2,)), dma, dma((2,)), dma, dma, dma((PARTS, groups)), dma, dma,
        ],
        compiler_params=pltpu.CompilerParams(
            collective_id=0, has_side_effects=True, vmem_limit_bytes=56 * 2**20
        ),
        cost_estimate=pl.CostEstimate(flops=13_000_000_000, bytes_accessed=8 * 2**20, transcendentals=8_400_000),
    )(query_raw, key_raw, values, query_tan, key_tan, values_tan,
      query_gain.reshape(1, share), key_gain.reshape(1, share))
    return pl.pallas_call(
        hand_out,
        out_shape=(jax.ShapeDtypeStruct((tok, width), BF16),) * 2,
        in_specs=[pl.BlockSpec(memory_space=pltpu.VMEM)],
        out_specs=(anywhere,) * 2,
        scratch_shapes=[dma((2,))],
    )(pltpu.with_memory_space_constraint(both, pltpu.VMEM))


def solution(mesh):
    tokens = P(("clip", "seq"), None)
    return jax.shard_map(
        on_device, mesh=mesh, in_specs=(tokens,) * 6 + (P("clip"),) * 2, out_specs=(tokens,) * 2, check_vma=False
    )
```

```python
import functools

import jax
import jax.numpy as jnp
from jax import lax
from jax.experimental import pallas as pl
from jax.experimental.pallas import tpu as pltpu
from jax.sharding import PartitionSpec as P

HEADS = 32
HD = 128
EPS = 1e-06
LOG2E = 1.4426950408889634
MESH = pl.DeviceIdType.MESH
F32 = jnp.float32
BF16 = jnp.bfloat16

FAR = ((3, 1), (2, 1), (1, 1), (0, 0))
NEAR = ((0, 1), (3, 0), (2, 0), (1, 0))
PLACES = tuple((dx, dy, core) for core in range(2) for chips in (FAR, NEAR) for dx, dy in chips)
OWN = PLACES.index((0, 0, 0))
OTHERS = tuple(p for p in range(16) if p != OWN)
PARTS = 2
CHUNKS = 4
RELAY = 0


def kernel(clips, q_hbm, k_hbm, v_hbm, qt_hbm, kt_hbm, vt_hbm, gq_hbm, gk_hbm, out_hbm,
           queries, keys, figures, figure_mine, figure_all, figure_of, gains, gain, handed_out,
           vbuf, vcat, kraw, kbuf, qbuf, obuf,
           load_k, load_q, gain_send, gain_recv, hand_send, hand_recv, figure_send, figure_recv,
           v_send, v_recv, k_send, k_recv, q_send, q_recv, o_send, o_recv):
    clip = lax.axis_index("clip")
    me = lax.axis_index("seq")
    x, y, core = me // 4, (me // 2) % 2, me % 2
    way = 1 - 2 * (x % 2)
    tok, width = q_hbm.shape
    groups = HEADS // 2
    length = groups * tok
    pair = 2 * HD
    piece = tok // PARTS
    share = gains.shape[-1]

    def at(place):
        dx, dy, other = PLACES[place]
        return ((x + way * dx + 4) % 4) * 4 + ((y + dy) % 2) * 2 + (core + other) % 2

    def visit(turn, act):
        group = (turn + 1 - core) % 4
        other, near = group // 2, group % 2
        for n in range(4):
            dx = FAR[n][0] + near * (NEAR[n][0] - FAR[n][0])
            dy = FAR[n][1] + near * (NEAR[n][1] - FAR[n][1])
            to = ((x + way * dx + 4) % 4) * 4 + ((y + dy) % 2) * 2 + (core + other) % 2
            act_here = functools.partial(act, group, n, to)
            if n == OWN % 4:
                pl.when(group != OWN // 4)(act_here)
            else:
                act_here()

    def rows_of(group, n):
        return pl.ds(pl.multiple_of((group * 4 + n) * tok, tok), tok)

    def columns(index, size):
        return pl.ds(pl.multiple_of(index * size, size), size)

    def send(src, dst, send_sem, recv_sem, to):
        pltpu.make_async_remote_copy(
            src_ref=src, dst_ref=dst, send_sem=send_sem, recv_sem=recv_sem, device_id=(clip, to), device_id_type=MESH).start()

    barrier = pltpu.get_barrier_semaphore()
    for place in OTHERS:
        pl.semaphore_signal(barrier, inc=1, device_id=(clip, at(place)), device_id_type=MESH)

    @pl.when(me == RELAY)
    def _():
        for step in range(1, clips):
            pl.semaphore_signal(barrier, inc=1, device_id=((clip + step) % clips, me), device_id_type=MESH)

    for i, src in enumerate((k_hbm, kt_hbm)):
        pltpu.make_async_copy(src, keys.at[i], load_k).start()
    for n in range(groups):
        for i, src in enumerate((qt_hbm, q_hbm)):
            pltpu.make_async_copy(
                src.at[:, n * pair:(n + 1) * pair], queries.at[:, (2 * n + i) * pair:(2 * n + i + 1) * pair], load_q).start()

    @pl.when(me != RELAY)
    def _():
        pl.semaphore_wait(barrier, len(OTHERS))

    @pl.when(me == RELAY)
    def _():
        pl.semaphore_wait(barrier, len(OTHERS) + clips - 1)
        for i, src in enumerate((gk_hbm, gq_hbm)):
            for step in range(1, clips):
                pltpu.make_async_remote_copy(
                    src_ref=src, dst_ref=gains.at[i, clip], send_sem=gain_send, recv_sem=gain_recv,
                    device_id=((clip + step) % clips, me), device_id_type=MESH).start()
            pltpu.make_async_copy(src, gains.at[i, clip], gain_recv).start()

    for i, src in enumerate((v_hbm, vt_hbm)):
        def give(group, n, to, i=i, src=src):
            send(src.at[:, columns(to, pair)], vbuf.at[i, rows_of(group, n), :], v_send, v_recv, to)

        for turn in range(4):
            visit(turn, give)
        pltpu.make_async_copy(src.at[:, columns(me, pair)], vbuf.at[i, pl.ds(OWN * tok, tok), :], v_recv).start()

    pltpu.make_async_copy(keys, keys, load_k).wait()
    pltpu.make_async_copy(queries, queries, load_q).wait()

    def token_figures(n, _):
        r = pl.ds(pl.multiple_of(n * 16, 16), 16)

        def pair_of(primal, tangent):
            square, cross = jnp.zeros((16, HD), F32), jnp.zeros((16, HD), F32)
            for h in range(HEADS):
                a, b = primal(h).astype(F32), tangent(h).astype(F32)
                square += a * a
                cross += a * b
            inverse = 1.0 / jnp.sqrt(jnp.sum(square, axis=1, keepdims=True) / width + EPS)
            return inverse, jnp.sum(cross, axis=1, keepdims=True) / width * (inverse * inverse * inverse)

        def query_part(i):
            def part(h):
                start = (2 * (h // 2) + i) * pair + h % 2 * HD
                return queries[r, start:start + HD]
            return part

        found = pair_of(query_part(1), query_part(0)) + pair_of(
            lambda h: keys[0, r, h * HD:(h + 1) * HD], lambda h: keys[1, r, h * HD:(h + 1) * HD])
        lane = lax.broadcasted_iota(jnp.int32, (16, HD), 1)
        row = jnp.zeros((16, HD), F32)
        for i, value in enumerate(found):
            row = jnp.where(lane == i, value, row)
        figures[r, :] = row
        return 0

    lax.fori_loop(0, tok // 16, token_figures, 0)
    figure_mine[...] = figures[...].T[:4, :]
    for place in OTHERS:
        send(figure_mine, figure_all.at[place], figure_send, figure_recv, at(place))
    pltpu.make_async_copy(figure_mine, figure_all.at[OWN], figure_recv).start()

    def gain_part(to):
        return gains.at[:, to // (share // pair), :, pl.ds(pl.multiple_of(to % (share // pair) * pair, pair), pair)]

    @pl.when(me == RELAY)
    def _():
        pltpu.make_async_copy(gains, gains, gain_recv).wait()
        for place in OTHERS:
            to = at(place)
            send(gain_part(to), gain, hand_send, hand_recv, to)
        pltpu.make_async_copy(gain_part(me), gain, hand_recv).start()

    for i in range(2):
        def give(group, n, to, i=i):
            send(keys.at[i, :, columns(to, pair)], kraw.at[i, rows_of(group, n), :], k_send, k_recv, to)

        for turn in range(4):
            visit(turn, give)
        pltpu.make_async_copy(keys.at[i, :, columns(me, pair)], kraw.at[i, pl.ds(OWN * tok, tok), :], k_recv).start()
    for part in range(PARTS):
        rows = pl.ds(part * piece, piece)

        def give(group, n, to, part=part, rows=rows):
            send(queries.at[rows, columns(to, 2 * pair)], qbuf.at[part, group, pl.ds(n * piece, piece), :],
                 q_send, q_recv.at[part, group], to)

        for turn in range(4):
            visit(turn, give)
        pltpu.make_async_copy(
            queries.at[rows, columns(me, 2 * pair)], qbuf.at[part, OWN // 4, pl.ds(OWN % 4 * piece, piece), :],
            q_recv.at[part, OWN // 4]).start()

    pltpu.make_async_copy(vbuf, vbuf, v_recv).wait()

    def interleave(n, _):
        r = pl.ds(pl.multiple_of(n * 128, 128), 128)
        for h in range(2):
            for i in range(2):
                vcat[r, (2 * h + i) * HD:(2 * h + i + 1) * HD] = vbuf[i, r, h * HD:(h + 1) * HD]
        return 0

    lax.fori_loop(0, length // 128, interleave, 0)
    pltpu.make_async_copy(figure_all, figure_all, figure_recv).wait()

    def upright(place, _):
        figure_of[place] = figure_all[place].T
        return 0

    lax.fori_loop(0, groups, upright, 0)
    pltpu.make_async_copy(gain, gain, hand_recv).wait()
    pltpu.make_async_copy(kraw, kraw, k_recv).wait()

    def norm(a, b, g, inverse, mixed):
        a, b = a.astype(F32), b.astype(F32)
        return (g * a * inverse).astype(BF16), (g * (b * inverse - a * mixed)).astype(BF16)

    def norm_keys(place, _):
        r = pl.ds(pl.multiple_of(place * tok, tok), tok)
        inverse, mixed = figure_of[place, :, 2:3], figure_of[place, :, 3:4]
        for h in range(2):
            cols = slice(h * HD, (h + 1) * HD)
            primal, tangent = norm(kraw[0, r, cols], kraw[1, r, cols], gain[0, :, cols], inverse, mixed)
            kbuf[h, r, :HD] = primal
            kbuf[h, r, HD:] = tangent
        return 0

    lax.fori_loop(0, groups, norm_keys, 0)

    scale = HD ** (-0.5)

    def attend(step, _):
        part, turn = step // 4, step % 4
        group = (turn + 1 - core) % 4
        rows = pl.ds(pl.multiple_of(part * piece, piece), piece)
        block = qbuf.at[part, group]
        pltpu.make_async_copy(block, block, q_recv.at[part, group]).wait()
        for h in range(2):
            primal, tangent = [], []
            for n in range(4):
                own = figure_of.at[group * 4 + n]
                p, t = norm(
                    qbuf[part, group, n * piece:(n + 1) * piece, pair + h * HD:pair + (h + 1) * HD],
                    qbuf[part, group, n * piece:(n + 1) * piece, h * HD:(h + 1) * HD],
                    gain[1, :, h * HD:(h + 1) * HD], own[rows, 0:1], own[rows, 1:2])
                primal.append(p)
                tangent.append(t)
            primal, tangent = jnp.concatenate(primal, axis=0), jnp.concatenate(tangent, axis=0)
            both_keys = kbuf[h]
            dims = (((1,), (1,)), ((), ()))
            scores = lax.dot_general(primal, both_keys[:, :HD], dims, preferred_element_type=F32)
            scores_tan = lax.dot_general(
                jnp.concatenate([tangent, primal], axis=1), both_keys, dims, preferred_element_type=F32)
            top = jnp.max(scores, axis=1, keepdims=True)
            weights = jnp.exp2((scores - top) * (scale * LOG2E))
            inverse = 1.0 / jnp.sum(weights, axis=1, keepdims=True)
            mean = jnp.sum(weights * scores_tan, axis=1, keepdims=True) * inverse
            low = (weights * inverse).astype(BF16)
            low_tan = (weights * (scores_tan - mean) * (inverse * scale)).astype(BF16)
            both = jnp.dot(low, vcat[:, h * pair:(h + 1) * pair], preferred_element_type=F32)
            rest = jnp.dot(low_tan, vcat[:, h * pair:h * pair + HD], preferred_element_type=F32)
            obuf[step, 0, :, h * HD:(h + 1) * HD] = both[:, :HD].astype(BF16)
            obuf[step, 1, :, h * HD:(h + 1) * HD] = (both[:, HD:] + rest).astype(BF16)

        def give(group, n, to):
            send(obuf.at[step, :, pl.ds(n * piece, piece), :], out_hbm.at[:, rows, columns(me, pair)], o_send, o_recv, to)

        visit(turn, give)

        @pl.when(group == OWN // 4)
        def _():
            pltpu.make_async_copy(
                obuf.at[step, :, pl.ds(OWN % 4 * piece, piece), :], out_hbm.at[:, rows, columns(me, pair)], o_recv).start()

        return 0

    lax.fori_loop(0, PARTS * 4, attend, 0)

    pltpu.make_async_copy(out_hbm, out_hbm, o_recv).wait()
    others = pl.ds(0, length - tok)
    pltpu.make_async_copy(vbuf.at[:, others, :], vbuf.at[:, others, :], v_send).wait()
    pltpu.make_async_copy(kraw.at[:, others, :], kraw.at[:, others, :], k_send).wait()
    pltpu.make_async_copy(figure_all.at[pl.ds(0, groups - 1)], figure_all.at[pl.ds(0, groups - 1)], figure_send).wait()
    most = pl.ds(0, 4 * piece - piece // 4)
    pltpu.make_async_copy(qbuf.at[:, :, most, :], qbuf.at[:, :, most, :], q_send).wait()
    pltpu.make_async_copy(obuf.at[:, :, most, :], obuf.at[:, :, most, :], o_send).wait()

    @pl.when(me == RELAY)
    def _():
        met = gains.at[:, pl.ds(0, clips - 1)]
        pltpu.make_async_copy(met, met, gain_send).wait()
        handed = handed_out.at[pl.ds(0, groups - 1)]
        pltpu.make_async_copy(handed, handed, hand_send).wait()


def hand_out(both, first, second, sems):
    rows = both.shape[1] // CHUNKS
    copies = [
        pltpu.make_async_copy(both.at[i, pl.ds(n * rows, rows), :], out.at[pl.ds(n * rows, rows), :], sems.at[i, n])
        for n in range(CHUNKS) for i, out in enumerate((first, second))]
    for copy in copies:
        copy.start()
    for copy in copies:
        copy.wait()


def on_device(query_raw, key_raw, values, query_tan, key_tan, values_tan, query_gain, key_gain):
    tok, width = query_raw.shape
    groups = lax.axis_size("seq")
    clips = lax.axis_size("clip")
    length = tok * groups
    share = query_gain.shape[0]
    pair = 2 * HD
    dma = pltpu.SemaphoreType.DMA
    anywhere = pl.BlockSpec(memory_space=pl.ANY)
    both = pl.pallas_call(
        functools.partial(kernel, clips),
        out_shape=pltpu.VMEM((2, tok, width), BF16),
        in_specs=[anywhere] * 8,
        out_specs=pl.BlockSpec(memory_space=pltpu.VMEM),
        scratch_shapes=[
            pltpu.VMEM((tok, 2 * width), BF16),
            pltpu.VMEM((2, tok, width), BF16),
            pltpu.VMEM((tok, HD), F32),
            pltpu.VMEM((4, tok), F32),
            pltpu.VMEM((groups, 4, tok), F32),
            pltpu.VMEM((groups, tok, 4), F32),
            pltpu.VMEM((2, clips, 1, share), F32),
            pltpu.VMEM((2, 1, pair), F32),
            pltpu.VMEM((groups, 2, 1, pair), F32),
            pltpu.VMEM((2, length, pair), BF16),
            pltpu.VMEM((length, 2 * pair), BF16),
            pltpu.VMEM((2, length, pair), BF16),
            pltpu.VMEM((2, length, pair), BF16),
            pltpu.VMEM((PARTS, 4, length // PARTS // 4, 2 * pair), BF16),
            pltpu.VMEM((PARTS * 4, 2, length // PARTS // 4, pair), BF16),
            dma, dma, dma, dma, dma, dma, dma, dma,
            dma, dma, dma, dma, dma, dma((PARTS, 4)), dma, dma,
        ],
        compiler_params=pltpu.CompilerParams(
            collective_id=0, has_side_effects=True, vmem_limit_bytes=56 * 2**20
        ),
        cost_estimate=pl.CostEstimate(flops=13_000_000_000, bytes_accessed=8 * 2**20, transcendentals=8_400_000),
    )(query_raw, key_raw, values, query_tan, key_tan, values_tan,
      query_gain.reshape(1, share), key_gain.reshape(1, share))
    return pl.pallas_call(
        hand_out,
        out_shape=(jax.ShapeDtypeStruct((tok, width), BF16),) * 2,
        in_specs=[pl.BlockSpec(memory_space=pltpu.VMEM)],
        out_specs=(anywhere,) * 2,
        scratch_shapes=[dma((2, CHUNKS))],
    )(pltpu.with_memory_space_constraint(both, pltpu.VMEM))


def solution(mesh):
    tokens = P(("clip", "seq"), None)
    return jax.shard_map(
        on_device, mesh=mesh, in_specs=(tokens,) * 6 + (P("clip"),) * 2, out_specs=(tokens,) * 2, check_vma=False
    )
```

```python
import functools

import jax
import jax.numpy as jnp
from jax import lax
from jax.experimental import pallas as pl
from jax.experimental.pallas import tpu as pltpu
from jax.sharding import PartitionSpec as P

HEADS = 32
HD = 128
EPS = 1e-06
LOG2E = 1.4426950408889634
MESH = pl.DeviceIdType.MESH
F32 = jnp.float32
BF16 = jnp.bfloat16

FAR = ((3, 1), (2, 1), (1, 1), (0, 0))
NEAR = ((0, 1), (3, 0), (2, 0), (1, 0))
PLACES = tuple((dx, dy, core) for core in range(2) for chips in (FAR, NEAR) for dx, dy in chips)
OWN = PLACES.index((0, 0, 0))
OTHERS = tuple(p for p in range(16) if p != OWN)
PARTS = 2
CHUNKS = 4
RELAY = 0


def kernel(clips, q_hbm, k_hbm, v_hbm, qt_hbm, kt_hbm, vt_hbm, gq_hbm, gk_hbm, out_hbm,
           queries, keys, figures, figure_mine, figure_all, figure_of, gains, gain, handed_out,
           vbuf, vcat, kraw, kbuf, qbuf, obuf,
           load_k, load_q, gain_send, gain_recv, hand_send, hand_recv, figure_send, figure_recv,
           v_send, v_recv, k_send, k_recv, q_send, q_recv, o_send, o_recv):
    clip = lax.axis_index("clip")
    me = lax.axis_index("seq")
    x, y, core = me // 4, (me // 2) % 2, me % 2
    way = 1 - 2 * (x % 2)
    tok, width = q_hbm.shape
    groups = HEADS // 2
    length = groups * tok
    pair = 2 * HD
    piece = tok // PARTS
    share = gains.shape[-1]

    def at(place):
        dx, dy, other = PLACES[place]
        return ((x + way * dx + 4) % 4) * 4 + ((y + dy) % 2) * 2 + (core + other) % 2

    def visit(turn, act):
        group = (turn + 1 - core) % 4
        other, near = group // 2, group % 2
        for n in range(4):
            dx = FAR[n][0] + near * (NEAR[n][0] - FAR[n][0])
            dy = FAR[n][1] + near * (NEAR[n][1] - FAR[n][1])
            to = ((x + way * dx + 4) % 4) * 4 + ((y + dy) % 2) * 2 + (core + other) % 2
            act_here = functools.partial(act, group, n, to)
            if n == OWN % 4:
                pl.when(group != OWN // 4)(act_here)
            else:
                act_here()

    def rows_of(group, n):
        return pl.ds(pl.multiple_of((group * 4 + n) * tok, tok), tok)

    def columns(index, size):
        return pl.ds(pl.multiple_of(index * size, size), size)

    def send(src, dst, send_sem, recv_sem, to):
        pltpu.make_async_remote_copy(
            src_ref=src, dst_ref=dst, send_sem=send_sem, recv_sem=recv_sem, device_id=(clip, to), device_id_type=MESH).start()

    barrier = pltpu.get_barrier_semaphore()
    for place in OTHERS:
        pl.semaphore_signal(barrier, inc=1, device_id=(clip, at(place)), device_id_type=MESH)

    @pl.when(me == RELAY)
    def _():
        for step in range(1, clips):
            pl.semaphore_signal(barrier, inc=1, device_id=((clip + step) % clips, me), device_id_type=MESH)

    for i, src in enumerate((k_hbm, kt_hbm)):
        pltpu.make_async_copy(src, keys.at[i], load_k).start()
    for i, src in enumerate((q_hbm, qt_hbm)):
        pltpu.make_async_copy(src, queries.at[i], load_q).start()

    @pl.when(me != RELAY)
    def _():
        pl.semaphore_wait(barrier, len(OTHERS))

    @pl.when(me == RELAY)
    def _():
        pl.semaphore_wait(barrier, len(OTHERS) + clips - 1)
        for i, src in enumerate((gk_hbm, gq_hbm)):
            for step in range(1, clips):
                pltpu.make_async_remote_copy(
                    src_ref=src, dst_ref=gains.at[i, clip], send_sem=gain_send, recv_sem=gain_recv,
                    device_id=((clip + step) % clips, me), device_id_type=MESH).start()
            pltpu.make_async_copy(src, gains.at[i, clip], gain_recv).start()

    for i, src in enumerate((v_hbm, vt_hbm)):
        def give(group, n, to, i=i, src=src):
            send(src.at[:, columns(to, pair)], vbuf.at[i, rows_of(group, n), :], v_send, v_recv, to)

        for turn in range(4):
            visit(turn, give)
        pltpu.make_async_copy(src.at[:, columns(me, pair)], vbuf.at[i, pl.ds(OWN * tok, tok), :], v_recv).start()

    pltpu.make_async_copy(keys, keys, load_k).wait()
    pltpu.make_async_copy(queries, queries, load_q).wait()

    def token_figures(n, _):
        r = pl.ds(pl.multiple_of(n * 16, 16), 16)

        def pair_of(primal, tangent):
            square, cross = jnp.zeros((16, HD), F32), jnp.zeros((16, HD), F32)
            for h in range(HEADS):
                a, b = primal(h).astype(F32), tangent(h).astype(F32)
                square += a * a
                cross += a * b
            inverse = 1.0 / jnp.sqrt(jnp.sum(square, axis=1, keepdims=True) / width + EPS)
            return inverse, jnp.sum(cross, axis=1, keepdims=True) / width * (inverse * inverse * inverse)

        def head_of(array, i):
            return lambda h: array[i, r, h * HD:(h + 1) * HD]

        found = pair_of(head_of(queries, 0), head_of(queries, 1)) + pair_of(head_of(keys, 0), head_of(keys, 1))
        lane = lax.broadcasted_iota(jnp.int32, (16, HD), 1)
        row = jnp.zeros((16, HD), F32)
        for i, value in enumerate(found):
            row = jnp.where(lane == i, value, row)
        figures[r, :] = row
        return 0

    lax.fori_loop(0, tok // 16, token_figures, 0)
    figure_mine[...] = figures[...].T[:4, :]
    for place in OTHERS:
        send(figure_mine, figure_all.at[place], figure_send, figure_recv, at(place))
    pltpu.make_async_copy(figure_mine, figure_all.at[OWN], figure_recv).start()

    def gain_part(to):
        return gains.at[:, to // (share // pair), :, pl.ds(pl.multiple_of(to % (share // pair) * pair, pair), pair)]

    @pl.when(me == RELAY)
    def _():
        pltpu.make_async_copy(gains, gains, gain_recv).wait()
        for place in OTHERS:
            to = at(place)
            send(gain_part(to), gain, hand_send, hand_recv, to)
        pltpu.make_async_copy(gain_part(me), gain, hand_recv).start()

    for i in range(2):
        def give(group, n, to, i=i):
            send(keys.at[i, :, columns(to, pair)], kraw.at[i, rows_of(group, n), :], k_send, k_recv, to)

        for turn in range(4):
            visit(turn, give)
        pltpu.make_async_copy(keys.at[i, :, columns(me, pair)], kraw.at[i, pl.ds(OWN * tok, tok), :], k_recv).start()
    for part in range(PARTS):
        rows = pl.ds(part * piece, piece)

        def give(group, n, to, part=part, rows=rows):
            send(queries.at[:, rows, columns(to, pair)], qbuf.at[part, group, :, pl.ds(n * piece, piece), :],
                 q_send, q_recv.at[part, group], to)

        for turn in range(4):
            visit(turn, give)
        pltpu.make_async_copy(
            queries.at[:, rows, columns(me, pair)], qbuf.at[part, OWN // 4, :, pl.ds(OWN % 4 * piece, piece), :],
            q_recv.at[part, OWN // 4]).start()

    pltpu.make_async_copy(vbuf, vbuf, v_recv).wait()

    def interleave(n, _):
        r = pl.ds(pl.multiple_of(n * 128, 128), 128)
        for h in range(2):
            for i in range(2):
                vcat[r, (2 * h + i) * HD:(2 * h + i + 1) * HD] = vbuf[i, r, h * HD:(h + 1) * HD]
        return 0

    lax.fori_loop(0, length // 128, interleave, 0)
    pltpu.make_async_copy(figure_all, figure_all, figure_recv).wait()

    def upright(place, _):
        figure_of[place] = figure_all[place].T
        return 0

    lax.fori_loop(0, groups, upright, 0)
    pltpu.make_async_copy(gain, gain, hand_recv).wait()
    pltpu.make_async_copy(kraw, kraw, k_recv).wait()

    def norm(a, b, g, inverse, mixed):
        a, b = a.astype(F32), b.astype(F32)
        return (g * a * inverse).astype(BF16), (g * (b * inverse - a * mixed)).astype(BF16)

    def norm_keys(place, _):
        r = pl.ds(pl.multiple_of(place * tok, tok), tok)
        inverse, mixed = figure_of[place, :, 2:3], figure_of[place, :, 3:4]
        for h in range(2):
            cols = slice(h * HD, (h + 1) * HD)
            primal, tangent = norm(kraw[0, r, cols], kraw[1, r, cols], gain[0, :, cols], inverse, mixed)
            kbuf[h, r, :HD] = primal
            kbuf[h, r, HD:] = tangent
        return 0

    lax.fori_loop(0, groups, norm_keys, 0)

    scale = HD ** (-0.5)

    def attend(step, _):
        part, turn = step // 4, step % 4
        group = (turn + 1 - core) % 4
        rows = pl.ds(pl.multiple_of(part * piece, piece), piece)
        block = qbuf.at[part, group]
        pltpu.make_async_copy(block, block, q_recv.at[part, group]).wait()
        for h in range(2):
            primal, tangent = [], []
            for n in range(4):
                own = figure_of.at[group * 4 + n]
                p, t = norm(
                    qbuf[part, group, 0, n * piece:(n + 1) * piece, h * HD:(h + 1) * HD],
                    qbuf[part, group, 1, n * piece:(n + 1) * piece, h * HD:(h + 1) * HD],
                    gain[1, :, h * HD:(h + 1) * HD], own[rows, 0:1], own[rows, 1:2])
                primal.append(p)
                tangent.append(t)
            primal, tangent = jnp.concatenate(primal, axis=0), jnp.concatenate(tangent, axis=0)
            both_keys = kbuf[h]
            dims = (((1,), (1,)), ((), ()))
            scores = lax.dot_general(primal, both_keys[:, :HD], dims, preferred_element_type=F32)
            scores_tan = lax.dot_general(
                jnp.concatenate([tangent, primal], axis=1), both_keys, dims, preferred_element_type=F32)
            top = jnp.max(scores, axis=1, keepdims=True)
            weights = jnp.exp2((scores - top) * (scale * LOG2E))
            inverse = 1.0 / jnp.sum(weights, axis=1, keepdims=True)
            mean = jnp.sum(weights * scores_tan, axis=1, keepdims=True) * inverse
            low = (weights * inverse).astype(BF16)
            low_tan = (weights * (scores_tan - mean) * (inverse * scale)).astype(BF16)
            both = jnp.dot(low, vcat[:, h * pair:(h + 1) * pair], preferred_element_type=F32)
            rest = jnp.dot(low_tan, vcat[:, h * pair:h * pair + HD], preferred_element_type=F32)
            obuf[step, 0, :, h * HD:(h + 1) * HD] = both[:, :HD].astype(BF16)
            obuf[step, 1, :, h * HD:(h + 1) * HD] = (both[:, HD:] + rest).astype(BF16)

        def give(group, n, to):
            send(obuf.at[step, :, pl.ds(n * piece, piece), :], out_hbm.at[:, rows, columns(me, pair)], o_send, o_recv, to)

        visit(turn, give)

        @pl.when(group == OWN // 4)
        def _():
            pltpu.make_async_copy(
                obuf.at[step, :, pl.ds(OWN % 4 * piece, piece), :], out_hbm.at[:, rows, columns(me, pair)], o_recv).start()

        return 0

    lax.fori_loop(0, PARTS * 4, attend, 0)

    pltpu.make_async_copy(out_hbm, out_hbm, o_recv).wait()
    others = pl.ds(0, length - tok)
    pltpu.make_async_copy(vbuf.at[:, others, :], vbuf.at[:, others, :], v_send).wait()
    pltpu.make_async_copy(kraw.at[:, others, :], kraw.at[:, others, :], k_send).wait()
    pltpu.make_async_copy(figure_all.at[pl.ds(0, groups - 1)], figure_all.at[pl.ds(0, groups - 1)], figure_send).wait()
    most = pl.ds(0, 4 * piece - piece // 4)
    pltpu.make_async_copy(qbuf.at[:, :, :, most, :], qbuf.at[:, :, :, most, :], q_send).wait()
    pltpu.make_async_copy(obuf.at[:, :, most, :], obuf.at[:, :, most, :], o_send).wait()

    @pl.when(me == RELAY)
    def _():
        met = gains.at[:, pl.ds(0, clips - 1)]
        pltpu.make_async_copy(met, met, gain_send).wait()
        handed = handed_out.at[pl.ds(0, groups - 1)]
        pltpu.make_async_copy(handed, handed, hand_send).wait()


def hand_out(both, first, second, sems):
    rows = both.shape[1] // CHUNKS
    copies = [
        pltpu.make_async_copy(both.at[i, pl.ds(n * rows, rows), :], out.at[pl.ds(n * rows, rows), :], sems.at[i, n])
        for n in range(CHUNKS) for i, out in enumerate((first, second))]
    for copy in copies:
        copy.start()
    for copy in copies:
        copy.wait()


def on_device(query_raw, key_raw, values, query_tan, key_tan, values_tan, query_gain, key_gain):
    tok, width = query_raw.shape
    groups = lax.axis_size("seq")
    clips = lax.axis_size("clip")
    length = tok * groups
    share = query_gain.shape[0]
    pair = 2 * HD
    dma = pltpu.SemaphoreType.DMA
    anywhere = pl.BlockSpec(memory_space=pl.ANY)
    both = pl.pallas_call(
        functools.partial(kernel, clips),
        out_shape=pltpu.VMEM((2, tok, width), BF16),
        in_specs=[anywhere] * 8,
        out_specs=pl.BlockSpec(memory_space=pltpu.VMEM),
        scratch_shapes=[
            pltpu.VMEM((2, tok, width), BF16),
            pltpu.VMEM((2, tok, width), BF16),
            pltpu.VMEM((tok, HD), F32),
            pltpu.VMEM((4, tok), F32),
            pltpu.VMEM((groups, 4, tok), F32),
            pltpu.VMEM((groups, tok, 4), F32),
            pltpu.VMEM((2, clips, 1, share), F32),
            pltpu.VMEM((2, 1, pair), F32),
            pltpu.VMEM((groups, 2, 1, pair), F32),
            pltpu.VMEM((2, length, pair), BF16),
            pltpu.VMEM((length, 2 * pair), BF16),
            pltpu.VMEM((2, length, pair), BF16),
            pltpu.VMEM((2, length, pair), BF16),
            pltpu.VMEM((PARTS, 4, 2, length // PARTS // 4, pair), BF16),
            pltpu.VMEM((PARTS * 4, 2, length // PARTS // 4, pair), BF16),
            dma, dma, dma, dma, dma, dma, dma, dma,
            dma, dma, dma, dma, dma, dma((PARTS, 4)), dma, dma,
        ],
        compiler_params=pltpu.CompilerParams(
            collective_id=0, has_side_effects=True, vmem_limit_bytes=56 * 2**20
        ),
        cost_estimate=pl.CostEstimate(flops=13_000_000_000, bytes_accessed=8 * 2**20, transcendentals=8_400_000),
    )(query_raw, key_raw, values, query_tan, key_tan, values_tan,
      query_gain.reshape(1, share), key_gain.reshape(1, share))
    return pl.pallas_call(
        hand_out,
        out_shape=(jax.ShapeDtypeStruct((tok, width), BF16),) * 2,
        in_specs=[pl.BlockSpec(memory_space=pltpu.VMEM)],
        out_specs=(anywhere,) * 2,
        scratch_shapes=[dma((2, CHUNKS))],
    )(pltpu.with_memory_space_constraint(both, pltpu.VMEM))


def solution(mesh):
    tokens = P(("clip", "seq"), None)
    return jax.shard_map(
        on_device, mesh=mesh, in_specs=(tokens,) * 6 + (P("clip"),) * 2, out_specs=(tokens,) * 2, check_vma=False
    )
```

```python
import functools

import jax
import jax.numpy as jnp
from jax import lax
from jax.experimental import pallas as pl
from jax.experimental.pallas import tpu as pltpu
from jax.sharding import PartitionSpec as P

HEADS = 32
HD = 128
EPS = 1e-06
LOG2E = 1.4426950408889634
MESH = pl.DeviceIdType.MESH
F32 = jnp.float32
BF16 = jnp.bfloat16

FAR = ((3, 1), (2, 1), (1, 1), (0, 0))
NEAR = ((0, 1), (3, 0), (2, 0), (1, 0))
PLACES = tuple((dx, dy, core) for core in range(2) for chips in (FAR, NEAR) for dx, dy in chips)
OWN = PLACES.index((0, 0, 0))
OTHERS = tuple(p for p in range(16) if p != OWN)
PARTS = 2
CHUNKS = 4
RELAY = 0


def kernel(clips, q_hbm, k_hbm, v_hbm, qt_hbm, kt_hbm, vt_hbm, gq_hbm, gk_hbm, out_hbm,
           queries, keys, figures, figure_mine, figure_all, figure_of, gains, gain, handed_out,
           vbuf, vcat, kraw, kbuf, qbuf, obuf,
           load_k, load_q, gain_send, gain_recv, hand_send, hand_recv, figure_send, figure_recv,
           v_send, v_recv, k_send, k_recv, q_send, q_recv, o_send, o_recv):
    clip = lax.axis_index("clip")
    me = lax.axis_index("seq")
    x, y, core = me // 4, (me // 2) % 2, me % 2
    way = 1 - 2 * (x % 2)
    tok, width = q_hbm.shape
    groups = HEADS // 2
    length = groups * tok
    pair = 2 * HD
    piece = tok // PARTS
    share = gains.shape[-1]

    def at(place):
        dx, dy, other = PLACES[place]
        return ((x + way * dx + 4) % 4) * 4 + ((y + dy) % 2) * 2 + (core + other) % 2

    def visit(turn, act):
        group = (turn + 1 - core) % 4
        other, near = group // 2, group % 2
        for n in range(4):
            dx = FAR[n][0] + near * (NEAR[n][0] - FAR[n][0])
            dy = FAR[n][1] + near * (NEAR[n][1] - FAR[n][1])
            to = ((x + way * dx + 4) % 4) * 4 + ((y + dy) % 2) * 2 + (core + other) % 2
            act_here = functools.partial(act, group, n, to)
            if n == OWN % 4:
                pl.when(group != OWN // 4)(act_here)
            else:
                act_here()

    def rows_of(group, n):
        return pl.ds(pl.multiple_of((group * 4 + n) * tok, tok), tok)

    def columns(index, size):
        return pl.ds(pl.multiple_of(index * size, size), size)

    def send(src, dst, send_sem, recv_sem, to):
        pltpu.make_async_remote_copy(
            src_ref=src, dst_ref=dst, send_sem=send_sem, recv_sem=recv_sem, device_id=(clip, to), device_id_type=MESH).start()

    barrier = pltpu.get_barrier_semaphore()
    for place in OTHERS:
        pl.semaphore_signal(barrier, inc=1, device_id=(clip, at(place)), device_id_type=MESH)

    @pl.when(me == RELAY)
    def _():
        for step in range(1, clips):
            pl.semaphore_signal(barrier, inc=1, device_id=((clip + step) % clips, me), device_id_type=MESH)

    @pl.when(me != RELAY)
    def _():
        pl.semaphore_wait(barrier, len(OTHERS))

    @pl.when(me == RELAY)
    def _():
        pl.semaphore_wait(barrier, len(OTHERS) + clips - 1)
        for i, src in enumerate((gk_hbm, gq_hbm)):
            for step in range(1, clips):
                pltpu.make_async_remote_copy(
                    src_ref=src, dst_ref=gains.at[i, clip], send_sem=gain_send, recv_sem=gain_recv,
                    device_id=((clip + step) % clips, me), device_id_type=MESH).start()
            pltpu.make_async_copy(src, gains.at[i, clip], gain_recv).start()

    for i, src in enumerate((v_hbm, vt_hbm)):
        def give(group, n, to, i=i, src=src):
            send(src.at[:, columns(to, pair)], vbuf.at[i, rows_of(group, n), :], v_send, v_recv, to)

        for turn in range(4):
            visit(turn, give)
        pltpu.make_async_copy(src.at[:, columns(me, pair)], vbuf.at[i, pl.ds(OWN * tok, tok), :], v_recv).start()

    for i, src in enumerate((k_hbm, kt_hbm)):
        pltpu.make_async_copy(src, keys.at[i], load_k).start()
    for i, src in enumerate((q_hbm, qt_hbm)):
        pltpu.make_async_copy(src, queries.at[i], load_q).start()

    pltpu.make_async_copy(keys, keys, load_k).wait()
    pltpu.make_async_copy(queries, queries, load_q).wait()

    def token_figures(n, _):
        r = pl.ds(pl.multiple_of(n * 16, 16), 16)

        def pair_of(primal, tangent):
            square, cross = jnp.zeros((16, HD), F32), jnp.zeros((16, HD), F32)
            for h in range(HEADS):
                a, b = primal(h).astype(F32), tangent(h).astype(F32)
                square += a * a
                cross += a * b
            inverse = 1.0 / jnp.sqrt(jnp.sum(square, axis=1, keepdims=True) / width + EPS)
            return inverse, jnp.sum(cross, axis=1, keepdims=True) / width * (inverse * inverse * inverse)

        def head_of(array, i):
            return lambda h: array[i, r, h * HD:(h + 1) * HD]

        found = pair_of(head_of(queries, 0), head_of(queries, 1)) + pair_of(head_of(keys, 0), head_of(keys, 1))
        lane = lax.broadcasted_iota(jnp.int32, (16, HD), 1)
        row = jnp.zeros((16, HD), F32)
        for i, value in enumerate(found):
            row = jnp.where(lane == i, value, row)
        figures[r, :] = row
        return 0

    lax.fori_loop(0, tok // 16, token_figures, 0)
    figure_mine[...] = figures[...].T[:4, :]
    for place in OTHERS:
        send(figure_mine, figure_all.at[place], figure_send, figure_recv, at(place))
    pltpu.make_async_copy(figure_mine, figure_all.at[OWN], figure_recv).start()

    def gain_part(to):
        return gains.at[:, to // (share // pair), :, pl.ds(pl.multiple_of(to % (share // pair) * pair, pair), pair)]

    @pl.when(me == RELAY)
    def _():
        pltpu.make_async_copy(gains, gains, gain_recv).wait()
        for place in OTHERS:
            to = at(place)
            send(gain_part(to), gain, hand_send, hand_recv, to)
        pltpu.make_async_copy(gain_part(me), gain, hand_recv).start()

    for i in range(2):
        def give(group, n, to, i=i):
            send(keys.at[i, :, columns(to, pair)], kraw.at[i, rows_of(group, n), :], k_send, k_recv, to)

        for turn in range(4):
            visit(turn, give)
        pltpu.make_async_copy(keys.at[i, :, columns(me, pair)], kraw.at[i, pl.ds(OWN * tok, tok), :], k_recv).start()
    for part in range(PARTS):
        rows = pl.ds(part * piece, piece)

        def give(group, n, to, part=part, rows=rows):
            send(queries.at[:, rows, columns(to, pair)], qbuf.at[part, group, :, pl.ds(n * piece, piece), :],
                 q_send, q_recv.at[part, group], to)

        for turn in range(4):
            visit(turn, give)
        pltpu.make_async_copy(
            queries.at[:, rows, columns(me, pair)], qbuf.at[part, OWN // 4, :, pl.ds(OWN % 4 * piece, piece), :],
            q_recv.at[part, OWN // 4]).start()

    pltpu.make_async_copy(vbuf, vbuf, v_recv).wait()

    def interleave(n, _):
        r = pl.ds(pl.multiple_of(n * 128, 128), 128)
        for h in range(2):
            for i in range(2):
                vcat[r, (2 * h + i) * HD:(2 * h + i + 1) * HD] = vbuf[i, r, h * HD:(h + 1) * HD]
        return 0

    lax.fori_loop(0, length // 128, interleave, 0)
    pltpu.make_async_copy(figure_all, figure_all, figure_recv).wait()

    def upright(place, _):
        figure_of[place] = figure_all[place].T
        return 0

    lax.fori_loop(0, groups, upright, 0)
    pltpu.make_async_copy(gain, gain, hand_recv).wait()
    pltpu.make_async_copy(kraw, kraw, k_recv).wait()

    def norm(a, b, g, inverse, mixed):
        a, b = a.astype(F32), b.astype(F32)
        return (g * a * inverse).astype(BF16), (g * (b * inverse - a * mixed)).astype(BF16)

    def norm_keys(place, _):
        r = pl.ds(pl.multiple_of(place * tok, tok), tok)
        inverse, mixed = figure_of[place, :, 2:3], figure_of[place, :, 3:4]
        for h in range(2):
            cols = slice(h * HD, (h + 1) * HD)
            primal, tangent = norm(kraw[0, r, cols], kraw[1, r, cols], gain[0, :, cols], inverse, mixed)
            kbuf[h, r, :HD] = primal
            kbuf[h, r, HD:] = tangent
        return 0

    lax.fori_loop(0, groups, norm_keys, 0)

    scale = HD ** (-0.5)

    def attend(step, _):
        part, turn = step // 4, step % 4
        group = (turn + 1 - core) % 4
        rows = pl.ds(pl.multiple_of(part * piece, piece), piece)
        block = qbuf.at[part, group]
        pltpu.make_async_copy(block, block, q_recv.at[part, group]).wait()
        for h in range(2):
            primal, tangent = [], []
            for n in range(4):
                own = figure_of.at[group * 4 + n]
                p, t = norm(
                    qbuf[part, group, 0, n * piece:(n + 1) * piece, h * HD:(h + 1) * HD],
                    qbuf[part, group, 1, n * piece:(n + 1) * piece, h * HD:(h + 1) * HD],
                    gain[1, :, h * HD:(h + 1) * HD], own[rows, 0:1], own[rows, 1:2])
                primal.append(p)
                tangent.append(t)
            primal, tangent = jnp.concatenate(primal, axis=0), jnp.concatenate(tangent, axis=0)
            both_keys = kbuf[h]
            dims = (((1,), (1,)), ((), ()))
            scores = lax.dot_general(primal, both_keys[:, :HD], dims, preferred_element_type=F32)
            scores_tan = lax.dot_general(
                jnp.concatenate([tangent, primal], axis=1), both_keys, dims, preferred_element_type=F32)
            top = jnp.max(scores, axis=1, keepdims=True)
            weights = jnp.exp2((scores - top) * (scale * LOG2E))
            inverse = 1.0 / jnp.sum(weights, axis=1, keepdims=True)
            mean = jnp.sum(weights * scores_tan, axis=1, keepdims=True) * inverse
            low = (weights * inverse).astype(BF16)
            low_tan = (weights * (scores_tan - mean) * (inverse * scale)).astype(BF16)
            both = jnp.dot(low, vcat[:, h * pair:(h + 1) * pair], preferred_element_type=F32)
            rest = jnp.dot(low_tan, vcat[:, h * pair:h * pair + HD], preferred_element_type=F32)
            obuf[step, 0, :, h * HD:(h + 1) * HD] = both[:, :HD].astype(BF16)
            obuf[step, 1, :, h * HD:(h + 1) * HD] = (both[:, HD:] + rest).astype(BF16)

        def give(group, n, to):
            send(obuf.at[step, :, pl.ds(n * piece, piece), :], out_hbm.at[:, rows, columns(me, pair)], o_send, o_recv, to)

        visit(turn, give)

        @pl.when(group == OWN // 4)
        def _():
            pltpu.make_async_copy(
                obuf.at[step, :, pl.ds(OWN % 4 * piece, piece), :], out_hbm.at[:, rows, columns(me, pair)], o_recv).start()

        return 0

    lax.fori_loop(0, PARTS * 4, attend, 0)

    pltpu.make_async_copy(out_hbm, out_hbm, o_recv).wait()
    others = pl.ds(0, length - tok)
    pltpu.make_async_copy(vbuf.at[:, others, :], vbuf.at[:, others, :], v_send).wait()
    pltpu.make_async_copy(kraw.at[:, others, :], kraw.at[:, others, :], k_send).wait()
    pltpu.make_async_copy(figure_all.at[pl.ds(0, groups - 1)], figure_all.at[pl.ds(0, groups - 1)], figure_send).wait()
    most = pl.ds(0, 4 * piece - piece // 4)
    pltpu.make_async_copy(qbuf.at[:, :, :, most, :], qbuf.at[:, :, :, most, :], q_send).wait()
    pltpu.make_async_copy(obuf.at[:, :, most, :], obuf.at[:, :, most, :], o_send).wait()

    @pl.when(me == RELAY)
    def _():
        met = gains.at[:, pl.ds(0, clips - 1)]
        pltpu.make_async_copy(met, met, gain_send).wait()
        handed = handed_out.at[pl.ds(0, groups - 1)]
        pltpu.make_async_copy(handed, handed, hand_send).wait()


def hand_out(both, first, second, sems):
    rows = both.shape[1] // CHUNKS
    copies = [
        pltpu.make_async_copy(both.at[i, pl.ds(n * rows, rows), :], out.at[pl.ds(n * rows, rows), :], sems.at[i, n])
        for n in range(CHUNKS) for i, out in enumerate((first, second))]
    for copy in copies:
        copy.start()
    for copy in copies:
        copy.wait()


def on_device(query_raw, key_raw, values, query_tan, key_tan, values_tan, query_gain, key_gain):
    tok, width = query_raw.shape
    groups = lax.axis_size("seq")
    clips = lax.axis_size("clip")
    length = tok * groups
    share = query_gain.shape[0]
    pair = 2 * HD
    dma = pltpu.SemaphoreType.DMA
    anywhere = pl.BlockSpec(memory_space=pl.ANY)
    both = pl.pallas_call(
        functools.partial(kernel, clips),
        out_shape=pltpu.VMEM((2, tok, width), BF16),
        in_specs=[anywhere] * 8,
        out_specs=pl.BlockSpec(memory_space=pltpu.VMEM),
        scratch_shapes=[
            pltpu.VMEM((2, tok, width), BF16),
            pltpu.VMEM((2, tok, width), BF16),
            pltpu.VMEM((tok, HD), F32),
            pltpu.VMEM((4, tok), F32),
            pltpu.VMEM((groups, 4, tok), F32),
            pltpu.VMEM((groups, tok, 4), F32),
            pltpu.VMEM((2, clips, 1, share), F32),
            pltpu.VMEM((2, 1, pair), F32),
            pltpu.VMEM((groups, 2, 1, pair), F32),
            pltpu.VMEM((2, length, pair), BF16),
            pltpu.VMEM((length, 2 * pair), BF16),
            pltpu.VMEM((2, length, pair), BF16),
            pltpu.VMEM((2, length, pair), BF16),
            pltpu.VMEM((PARTS, 4, 2, length // PARTS // 4, pair), BF16),
            pltpu.VMEM((PARTS * 4, 2, length // PARTS // 4, pair), BF16),
            dma, dma, dma, dma, dma, dma, dma, dma,
            dma, dma, dma, dma, dma, dma((PARTS, 4)), dma, dma,
        ],
        compiler_params=pltpu.CompilerParams(
            collective_id=0, has_side_effects=True, vmem_limit_bytes=56 * 2**20
        ),
        cost_estimate=pl.CostEstimate(flops=13_000_000_000, bytes_accessed=8 * 2**20, transcendentals=8_400_000),
    )(query_raw, key_raw, values, query_tan, key_tan, values_tan,
      query_gain.reshape(1, share), key_gain.reshape(1, share))
    return pl.pallas_call(
        hand_out,
        out_shape=(jax.ShapeDtypeStruct((tok, width), BF16),) * 2,
        in_specs=[pl.BlockSpec(memory_space=pltpu.VMEM)],
        out_specs=(anywhere,) * 2,
        scratch_shapes=[dma((2, CHUNKS))],
    )(pltpu.with_memory_space_constraint(both, pltpu.VMEM))


def solution(mesh):
    tokens = P(("clip", "seq"), None)
    return jax.shard_map(
        on_device, mesh=mesh, in_specs=(tokens,) * 6 + (P("clip"),) * 2, out_specs=(tokens,) * 2, check_vma=False
    )
```

```python
import functools

import jax
import jax.numpy as jnp
from jax import lax
from jax.experimental import pallas as pl
from jax.experimental.pallas import tpu as pltpu
from jax.sharding import PartitionSpec as P

HEADS = 32
HD = 128
EPS = 1e-06
LOG2E = 1.4426950408889634
MESH = pl.DeviceIdType.MESH
F32 = jnp.float32
BF16 = jnp.bfloat16

FAR = ((3, 1), (2, 1), (1, 1), (0, 0))
NEAR = ((0, 1), (3, 0), (2, 0), (1, 0))
PLACES = tuple((dx, dy, core) for core in range(2) for chips in (FAR, NEAR) for dx, dy in chips)
OWN = PLACES.index((0, 0, 0))
OTHERS = tuple(p for p in range(16) if p != OWN)
PARTS = 2
CHUNKS = 1
RELAY = 0


def kernel(clips, q_hbm, k_hbm, v_hbm, qt_hbm, kt_hbm, vt_hbm, gq_hbm, gk_hbm, out_hbm,
           queries, keys, figures, figure_mine, figure_all, figure_of, gains, gain, handed_out,
           vbuf, vcat, kraw, kbuf, qbuf, obuf,
           load_k, load_q, gain_send, gain_recv, hand_send, hand_recv, figure_send, figure_recv,
           v_send, v_recv, k_send, k_recv, q_send, q_recv, o_send, o_recv):
    clip = lax.axis_index("clip")
    me = lax.axis_index("seq")
    x, y, core = me // 4, (me // 2) % 2, me % 2
    way = 1 - 2 * (x % 2)
    tok, width = q_hbm.shape
    groups = HEADS // 2
    length = groups * tok
    pair = 2 * HD
    piece = tok // PARTS
    share = gains.shape[-1]

    def at(place):
        dx, dy, other = PLACES[place]
        return ((x + way * dx + 4) % 4) * 4 + ((y + dy) % 2) * 2 + (core + other) % 2

    def visit(turn, act):
        group = (turn + 1 - core) % 4
        other, near = group // 2, group % 2
        for n in range(4):
            dx = FAR[n][0] + near * (NEAR[n][0] - FAR[n][0])
            dy = FAR[n][1] + near * (NEAR[n][1] - FAR[n][1])
            to = ((x + way * dx + 4) % 4) * 4 + ((y + dy) % 2) * 2 + (core + other) % 2
            act_here = functools.partial(act, group, n, to)
            if n == OWN % 4:
                pl.when(group != OWN // 4)(act_here)
            else:
                act_here()

    def rows_of(group, n):
        return pl.ds(pl.multiple_of((group * 4 + n) * tok, tok), tok)

    def columns(index, size):
        return pl.ds(pl.multiple_of(index * size, size), size)

    def send(src, dst, send_sem, recv_sem, to):
        pltpu.make_async_remote_copy(
            src_ref=src, dst_ref=dst, send_sem=send_sem, recv_sem=recv_sem, device_id=(clip, to), device_id_type=MESH).start()

    barrier = pltpu.get_barrier_semaphore()
    for place in OTHERS:
        pl.semaphore_signal(barrier, inc=1, device_id=(clip, at(place)), device_id_type=MESH)

    @pl.when(me == RELAY)
    def _():
        for step in range(1, clips):
            pl.semaphore_signal(barrier, inc=1, device_id=((clip + step) % clips, me), device_id_type=MESH)

    @pl.when(me != RELAY)
    def _():
        pl.semaphore_wait(barrier, len(OTHERS))

    @pl.when(me == RELAY)
    def _():
        pl.semaphore_wait(barrier, len(OTHERS) + clips - 1)
        for i, src in enumerate((gk_hbm, gq_hbm)):
            for step in range(1, clips):
                pltpu.make_async_remote_copy(
                    src_ref=src, dst_ref=gains.at[i, clip], send_sem=gain_send, recv_sem=gain_recv,
                    device_id=((clip + step) % clips, me), device_id_type=MESH).start()
            pltpu.make_async_copy(src, gains.at[i, clip], gain_recv).start()

    for i, src in enumerate((v_hbm, vt_hbm)):
        def give(group, n, to, i=i, src=src):
            send(src.at[:, columns(to, pair)], vbuf.at[i, rows_of(group, n), :], v_send, v_recv, to)

        for turn in range(4):
            visit(turn, give)
        pltpu.make_async_copy(src.at[:, columns(me, pair)], vbuf.at[i, pl.ds(OWN * tok, tok), :], v_recv).start()

    for i, src in enumerate((k_hbm, kt_hbm)):
        pltpu.make_async_copy(src, keys.at[i], load_k).start()
    for i, src in enumerate((q_hbm, qt_hbm)):
        pltpu.make_async_copy(src, queries.at[i], load_q).start()

    pltpu.make_async_copy(keys, keys, load_k).wait()
    pltpu.make_async_copy(queries, queries, load_q).wait()

    def token_figures(n, _):
        r = pl.ds(pl.multiple_of(n * 16, 16), 16)

        def pair_of(primal, tangent):
            square, cross = jnp.zeros((16, HD), F32), jnp.zeros((16, HD), F32)
            for h in range(HEADS):
                a, b = primal(h).astype(F32), tangent(h).astype(F32)
                square += a * a
                cross += a * b
            inverse = 1.0 / jnp.sqrt(jnp.sum(square, axis=1, keepdims=True) / width + EPS)
            return inverse, jnp.sum(cross, axis=1, keepdims=True) / width * (inverse * inverse * inverse)

        def head_of(array, i):
            return lambda h: array[i, r, h * HD:(h + 1) * HD]

        found = pair_of(head_of(queries, 0), head_of(queries, 1)) + pair_of(head_of(keys, 0), head_of(keys, 1))
        lane = lax.broadcasted_iota(jnp.int32, (16, HD), 1)
        row = jnp.zeros((16, HD), F32)
        for i, value in enumerate(found):
            row = jnp.where(lane == i, value, row)
        figures[r, :] = row
        return 0

    lax.fori_loop(0, tok // 16, token_figures, 0)
    figure_mine[...] = figures[...].T[:4, :]
    for place in OTHERS:
        send(figure_mine, figure_all.at[place], figure_send, figure_recv, at(place))
    pltpu.make_async_copy(figure_mine, figure_all.at[OWN], figure_recv).start()

    def gain_part(to):
        return gains.at[:, to // (share // pair), :, pl.ds(pl.multiple_of(to % (share // pair) * pair, pair), pair)]

    @pl.when(me == RELAY)
    def _():
        pltpu.make_async_copy(gains, gains, gain_recv).wait()
        for place in OTHERS:
            to = at(place)
            send(gain_part(to), gain, hand_send, hand_recv, to)
        pltpu.make_async_copy(gain_part(me), gain, hand_recv).start()

    for i in range(2):
        def give(group, n, to, i=i):
            send(keys.at[i, :, columns(to, pair)], kraw.at[i, rows_of(group, n), :], k_send, k_recv, to)

        for turn in range(4):
            visit(turn, give)
        pltpu.make_async_copy(keys.at[i, :, columns(me, pair)], kraw.at[i, pl.ds(OWN * tok, tok), :], k_recv).start()
    for part in range(PARTS):
        rows = pl.ds(part * piece, piece)

        def give(group, n, to, part=part, rows=rows):
            send(queries.at[:, rows, columns(to, pair)], qbuf.at[part, group, :, pl.ds(n * piece, piece), :],
                 q_send, q_recv.at[part, group], to)

        for turn in range(4):
            visit(turn, give)
        pltpu.make_async_copy(
            queries.at[:, rows, columns(me, pair)], qbuf.at[part, OWN // 4, :, pl.ds(OWN % 4 * piece, piece), :],
            q_recv.at[part, OWN // 4]).start()

    pltpu.make_async_copy(vbuf, vbuf, v_recv).wait()

    def interleave(n, _):
        r = pl.ds(pl.multiple_of(n * 128, 128), 128)
        for h in range(2):
            for i in range(2):
                vcat[r, (2 * h + i) * HD:(2 * h + i + 1) * HD] = vbuf[i, r, h * HD:(h + 1) * HD]
        return 0

    lax.fori_loop(0, length // 128, interleave, 0)
    pltpu.make_async_copy(figure_all, figure_all, figure_recv).wait()

    def upright(place, _):
        figure_of[place] = figure_all[place].T
        return 0

    lax.fori_loop(0, groups, upright, 0)
    pltpu.make_async_copy(gain, gain, hand_recv).wait()
    pltpu.make_async_copy(kraw, kraw, k_recv).wait()

    def norm(a, b, g, inverse, mixed):
        a, b = a.astype(F32), b.astype(F32)
        return (g * a * inverse).astype(BF16), (g * (b * inverse - a * mixed)).astype(BF16)

    def norm_keys(place, _):
        r = pl.ds(pl.multiple_of(place * tok, tok), tok)
        inverse, mixed = figure_of[place, :, 2:3], figure_of[place, :, 3:4]
        for h in range(2):
            cols = slice(h * HD, (h + 1) * HD)
            primal, tangent = norm(kraw[0, r, cols], kraw[1, r, cols], gain[0, :, cols], inverse, mixed)
            kbuf[h, r, :HD] = primal
            kbuf[h, r, HD:] = tangent
        return 0

    lax.fori_loop(0, groups, norm_keys, 0)

    scale = HD ** (-0.5)

    def attend(step, _):
        part, turn = step // 4, step % 4
        group = (turn + 1 - core) % 4
        rows = pl.ds(pl.multiple_of(part * piece, piece), piece)
        block = qbuf.at[part, group]
        pltpu.make_async_copy(block, block, q_recv.at[part, group]).wait()
        for h in range(2):
            primal, tangent = [], []
            for n in range(4):
                own = figure_of.at[group * 4 + n]
                p, t = norm(
                    qbuf[part, group, 0, n * piece:(n + 1) * piece, h * HD:(h + 1) * HD],
                    qbuf[part, group, 1, n * piece:(n + 1) * piece, h * HD:(h + 1) * HD],
                    gain[1, :, h * HD:(h + 1) * HD], own[rows, 0:1], own[rows, 1:2])
                primal.append(p)
                tangent.append(t)
            primal, tangent = jnp.concatenate(primal, axis=0), jnp.concatenate(tangent, axis=0)
            both_keys = kbuf[h]
            dims = (((1,), (1,)), ((), ()))
            scores = lax.dot_general(primal, both_keys[:, :HD], dims, preferred_element_type=F32)
            scores_tan = lax.dot_general(
                jnp.concatenate([tangent, primal], axis=1), both_keys, dims, preferred_element_type=F32)
            top = jnp.max(scores, axis=1, keepdims=True)
            weights = jnp.exp2((scores - top) * (scale * LOG2E))
            inverse = 1.0 / jnp.sum(weights, axis=1, keepdims=True)
            mean = jnp.sum(weights * scores_tan, axis=1, keepdims=True) * inverse
            low = (weights * inverse).astype(BF16)
            low_tan = (weights * (scores_tan - mean) * (inverse * scale)).astype(BF16)
            both = jnp.dot(low, vcat[:, h * pair:(h + 1) * pair], preferred_element_type=F32)
            rest = jnp.dot(low_tan, vcat[:, h * pair:h * pair + HD], preferred_element_type=F32)
            obuf[step, 0, :, h * HD:(h + 1) * HD] = both[:, :HD].astype(BF16)
            obuf[step, 1, :, h * HD:(h + 1) * HD] = (both[:, HD:] + rest).astype(BF16)

        def give(group, n, to):
            send(obuf.at[step, :, pl.ds(n * piece, piece), :], out_hbm.at[:, rows, columns(me, pair)], o_send, o_recv, to)

        visit(turn, give)

        @pl.when(group == OWN // 4)
        def _():
            pltpu.make_async_copy(
                obuf.at[step, :, pl.ds(OWN % 4 * piece, piece), :], out_hbm.at[:, rows, columns(me, pair)], o_recv).start()

        return 0

    lax.fori_loop(0, PARTS * 4, attend, 0)

    pltpu.make_async_copy(out_hbm, out_hbm, o_recv).wait()
    others = pl.ds(0, length - tok)
    pltpu.make_async_copy(vbuf.at[:, others, :], vbuf.at[:, others, :], v_send).wait()
    pltpu.make_async_copy(kraw.at[:, others, :], kraw.at[:, others, :], k_send).wait()
    pltpu.make_async_copy(figure_all.at[pl.ds(0, groups - 1)], figure_all.at[pl.ds(0, groups - 1)], figure_send).wait()
    most = pl.ds(0, 4 * piece - piece // 4)
    pltpu.make_async_copy(qbuf.at[:, :, :, most, :], qbuf.at[:, :, :, most, :], q_send).wait()
    pltpu.make_async_copy(obuf.at[:, :, most, :], obuf.at[:, :, most, :], o_send).wait()

    @pl.when(me == RELAY)
    def _():
        met = gains.at[:, pl.ds(0, clips - 1)]
        pltpu.make_async_copy(met, met, gain_send).wait()
        handed = handed_out.at[pl.ds(0, groups - 1)]
        pltpu.make_async_copy(handed, handed, hand_send).wait()


def hand_out(both, first, second, sems):
    rows = both.shape[1] // CHUNKS
    copies = [
        pltpu.make_async_copy(both.at[i, pl.ds(n * rows, rows), :], out.at[pl.ds(n * rows, rows), :], sems.at[i, n])
        for n in range(CHUNKS) for i, out in enumerate((first, second))]
    for copy in copies:
        copy.start()
    for copy in copies:
        copy.wait()


def on_device(query_raw, key_raw, values, query_tan, key_tan, values_tan, query_gain, key_gain):
    tok, width = query_raw.shape
    groups = lax.axis_size("seq")
    clips = lax.axis_size("clip")
    length = tok * groups
    share = query_gain.shape[0]
    pair = 2 * HD
    dma = pltpu.SemaphoreType.DMA
    anywhere = pl.BlockSpec(memory_space=pl.ANY)
    both = pl.pallas_call(
        functools.partial(kernel, clips),
        out_shape=pltpu.VMEM((2, tok, width), BF16),
        in_specs=[anywhere] * 8,
        out_specs=pl.BlockSpec(memory_space=pltpu.VMEM),
        scratch_shapes=[
            pltpu.VMEM((2, tok, width), BF16),
            pltpu.VMEM((2, tok, width), BF16),
            pltpu.VMEM((tok, HD), F32),
            pltpu.VMEM((4, tok), F32),
            pltpu.VMEM((groups, 4, tok), F32),
            pltpu.VMEM((groups, tok, 4), F32),
            pltpu.VMEM((2, clips, 1, share), F32),
            pltpu.VMEM((2, 1, pair), F32),
            pltpu.VMEM((groups, 2, 1, pair), F32),
            pltpu.VMEM((2, length, pair), BF16),
            pltpu.VMEM((length, 2 * pair), BF16),
            pltpu.VMEM((2, length, pair), BF16),
            pltpu.VMEM((2, length, pair), BF16),
            pltpu.VMEM((PARTS, 4, 2, length // PARTS // 4, pair), BF16),
            pltpu.VMEM((PARTS * 4, 2, length // PARTS // 4, pair), BF16),
            dma, dma, dma, dma, dma, dma, dma, dma,
            dma, dma, dma, dma, dma, dma((PARTS, 4)), dma, dma,
        ],
        compiler_params=pltpu.CompilerParams(
            collective_id=0, has_side_effects=True, vmem_limit_bytes=56 * 2**20
        ),
        cost_estimate=pl.CostEstimate(flops=13_000_000_000, bytes_accessed=8 * 2**20, transcendentals=8_400_000),
    )(query_raw, key_raw, values, query_tan, key_tan, values_tan,
      query_gain.reshape(1, share), key_gain.reshape(1, share))
    return pl.pallas_call(
        hand_out,
        out_shape=(jax.ShapeDtypeStruct((tok, width), BF16),) * 2,
        in_specs=[pl.BlockSpec(memory_space=pltpu.VMEM)],
        out_specs=(anywhere,) * 2,
        scratch_shapes=[dma((2, CHUNKS))],
    )(pltpu.with_memory_space_constraint(both, pltpu.VMEM))


def solution(mesh):
    tokens = P(("clip", "seq"), None)
    return jax.shard_map(
        on_device, mesh=mesh, in_specs=(tokens,) * 6 + (P("clip"),) * 2, out_specs=(tokens,) * 2, check_vma=False
    )
```
